512 devices in a mesh: nodes: 8 (over z_lo, core), space: 64 (over x, z_hi, y).
Axes of the slice: x: 4, y: 4, z: 16 (z_hi: 4, z_lo: 4; z = z_hi * 4 + z_lo), core: 2. Of those that a mesh axis runs over, the one named last changes fastest.
Arguments:
- displacement: float32 [32, 3, 256, 64, 256], P('nodes', None, 'space'), may hold values from -4 to 4
- slot_node: int32 [32], P('nodes'), may hold values from 0 to 31, each once
- node_weight: float32 [25], replicated, may hold values from -0.05 to 0.12
- node_stiffness: float32 [25], replicated, may hold values from 0.5 to 2
- design: float32 [256, 64, 256], P('space', 'nodes'), may hold values from 0.05 to 0.95
Outputs:
- gradient: float32 [256, 64, 256], P('space', 'nodes')
The draws below stay inside these ranges and needn't reach their ends.
Inputs may be any that keep to these rules, and one draw needn't show every extreme that they name: `slot_node`: every node 0 to 24 is held by exactly one slot; values of 25 or more mark empty slots.
All inputs are finite; a program needn't handle non-finite values.
Results may differ from the reference program's by a relative error of at most 0.0001.
Values sent between devices are 32-bit elements; how exact they have to be, the bound alone decides.
A program may use at most 128 MiB of HBM per device.

```python
import math
import jax
import jax.numpy as jnp
import numpy as np
from jax import lax

NODES = 25
NY = 64
NX = 256
SLOTS = 32
NZ = 256


def block_levels(stream_key, shape, shards, smallest, largest):
    gain = 1.0
    for axis_at, shards_of in shards:
        steps = jax.random.uniform(jax.random.fold_in(jax.random.fold_in(stream_key, 6), axis_at), (shards_of,), jnp.float32, smallest / len(shards), largest / len(shards))
        gain = gain * jnp.repeat(jnp.exp(steps), shape[axis_at] // shards_of).reshape((-1,) + (1,) * (len(shape) - 1 - axis_at))
    return gain


def bell_draw(own_key, shape, scale, most, split=(), kind=jnp.bfloat16):
    array = jax.random.normal(own_key, shape, jnp.float32) * scale
    if len(split) > 0:
        array = block_levels(own_key, shape, split, -0.22, 0.18) * array
    return jnp.clip(array, min=-most, max=most).astype(kind)


def setup_inputs(seed: int = 0) -> dict:
    streams_of = jax.random.split(jax.random.key(seed), 6)
    return {
        "displacement": bell_draw(streams_of[0], (SLOTS, 3, NZ, NY, NX), 0.5, 4.0, ((0, 8), (2, 64)), jnp.float32),
        "slot_node": jax.random.permutation(streams_of[1], SLOTS).astype(jnp.int32),
        "node_weight": jnp.clip(jax.random.uniform(streams_of[2], (NODES,), jnp.float32, -0.05, 0.12), -0.05, 0.12),
        "node_stiffness": jnp.clip(jnp.exp(jax.random.uniform(streams_of[3], (NODES,), jnp.float32, math.log(0.5), math.log(2.0))), 0.5, 2.0),
        "design": jnp.clip(0.05 + 0.9 * jax.random.uniform(streams_of[4], (NZ, NY, NX), jnp.float32) ** block_levels(streams_of[4], (NZ, NY, NX), ((0, 64), (1, 8)), -0.2, 0.2), 0.05, 0.95),
    }


POISSON = 0.3
E_FLOOR = 0.001
BETA = 8.0
ETA = 0.5

def element_matrix():
    lam = POISSON / ((1.0 + POISSON) * (1.0 - 2.0 * POISSON))
    shear = 1.0 / (2.0 * (1.0 + POISSON))
    elastic = np.zeros((6, 6))
    elastic[:3, :3] = lam
    elastic[:3, :3] += 2.0 * shear * np.eye(3)
    elastic[3:, 3:] = shear * np.eye(3)
    point = 1.0 / math.sqrt(3.0)
    stiff = np.zeros((24, 24))
    for gz in (-point, point):
        for gy in (-point, point):
            for gx in (-point, point):
                strain = np.zeros((6, 24))
                for corner in range(8):
                    sx = 2 * (corner % 2) - 1
                    sy = 2 * (corner // 2 % 2) - 1
                    sz = 2 * (corner // 4) - 1
                    fx = (1 + sx * gx) / 2
                    fy = (1 + sy * gy) / 2
                    fz = (1 + sz * gz) / 2
                    dnx = sx * fy * fz
                    dny = sy * fx * fz
                    dnz = sz * fx * fy
                    col = 3 * corner
                    strain[0, col] = dnx
                    strain[1, col + 1] = dny
                    strain[2, col + 2] = dnz
                    strain[3, col + 1] = dnz
                    strain[3, col + 2] = dny
                    strain[4, col] = dnz
                    strain[4, col + 2] = dnx
                    strain[5, col] = dny
                    strain[5, col + 1] = dnx
                stiff += strain.T @ elastic @ strain / 8.0
    return np.asarray(stiff, np.float32)

def filter_offsets():
    found = []
    for dz in range(-2, 3):
        for dy in range(-2, 3):
            for dx in range(-2, 3):
                dist = math.sqrt(dz * dz + dy * dy + dx * dx)
                if dist < 2.5:
                    found.append((dz, dy, dx, 2.5 - dist))
    return found

def smooth(padded, planes, rows, cols):
    total = jnp.zeros((planes, rows, cols), jnp.float32)
    for dz, dy, dx, weight in filter_offsets():
        total = total + weight * padded[2 + dz:2 + dz + planes, 2 + dy:2 + dy + rows, 2 + dx:2 + dx + cols]
    return total

def project(filtered):
    base = math.tanh(BETA * ETA)
    scale = base + math.tanh(BETA * (1.0 - ETA))
    level = jnp.tanh(BETA * (filtered - ETA))
    return ((base + level) / scale, BETA * (1.0 - level * level) / scale)

def element_energy(field, stiffness):
    planes = field.shape[1] - 1
    rows = field.shape[2] - 1
    cols = field.shape[3] - 1
    pieces = []
    for corner in range(8):
        a = corner % 2
        b = corner // 2 % 2
        c = corner // 4
        pieces.append(field[:, c:c + planes, b:b + rows, a:a + cols])
    vector = jnp.stack(pieces).reshape(24, planes * rows * cols)
    image = jnp.dot(stiffness, vector, precision=lax.Precision.HIGHEST, preferred_element_type=jnp.float32)
    return lax.optimization_barrier(jnp.sum(vector * image, axis=0)).reshape(planes, rows, cols)

def reference(displacement, slot_node, node_weight, node_stiffness, design):
    stiffness = jnp.asarray(element_matrix())
    planes, rows, cols = design.shape
    cover = smooth(jnp.pad(jnp.ones((planes, rows, cols), jnp.float32), 2), planes, rows, cols)
    filtered = smooth(jnp.pad(design, 2), planes, rows, cols) / cover
    projected, slope = project(filtered)
    picks = (slot_node[:, None] == jnp.arange(NODES, dtype=jnp.int32)[None, :]).astype(jnp.float32)
    coef = lax.optimization_barrier(jnp.sum(picks * (node_weight * node_stiffness)[None, :], axis=1))

    def add_slot(slot, total):
        field = lax.dynamic_index_in_dim(displacement, slot, 0, keepdims=False)
        field = jnp.pad(field, ((0, 0), (0, 1), (0, 1), (0, 1)))
        return total + coef[slot] * element_energy(field, stiffness)
    total = lax.fori_loop(0, displacement.shape[0], add_slot, jnp.zeros((planes, rows, cols), jnp.float32))
    sens = -3.0 * (1.0 - E_FLOOR) * (projected * projected) * total
    return smooth(jnp.pad(sens * slope / cover, 2), planes, rows, cols)
```

```python
import math

import jax
import jax.numpy as jnp
from jax import lax
from jax.experimental import pallas as pl
from jax.experimental.pallas import tpu as pltpu
from jax.sharding import PartitionSpec as P

POISSON = 0.3
E_FLOOR = 0.001
BETA = 8.0
ETA = 0.5
RADIUS = 2.5
MESH = pl.DeviceIdType.MESH


def weight(dz, dy, dx):
    return max(0.0, RADIUS - math.sqrt(dz * dz + dy * dy + dx * dx))


def add_up(terms):
    total = None
    for term in terms:
        total = term if total is None else total + term
    return total


def next_lane(v, last):
    return jnp.where(last, 0.0, pltpu.roll(v, v.shape[1] - 1, 1))


def plane_modes(load, next_rows, last):
    modes = []
    for comp in range(3):
        here, below = load(comp)
        up = pltpu.roll(jnp.where(next_rows, below, here), 7, 0)
        ysum, ydif = up + here, up - here
        ysum_x, ydif_x = next_lane(ysum, last), next_lane(ydif, last)
        modes.append((ysum_x + ysum, ysum_x - ysum, ydif_x + ydif, ydif_x - ydif))
    return modes


def layer_energy(low, high):
    lam = POISSON / ((1.0 + POISSON) * (1.0 - 2.0 * POISSON))
    shear = 1.0 / (2.0 * (1.0 + POISSON))
    sums = [[lo + hi for lo, hi in zip(a, b)] for a, b in zip(low, high)]
    difs = [[hi - lo for lo, hi in zip(a, b)] for a, b in zip(low, high)]
    (_, ax, ay, axy), (_, bx, by, bxy), (_, cx, cy, cxy) = sums
    (az, azx, ayz, axyz), (bz, bzx, byz, bxyz), (cz, czx, cyz, cxyz) = difs
    sq = lambda v: v * v
    div = sq(ax + by + cz)
    diag = sq(ax) + sq(by) + sq(cz)
    skew = sq(ay + bx) + sq(az + cx) + sq(bz + cy)
    even = sq(bxy + czx) + sq(axy + cyz) + sq(azx + byz)
    odd = sq(bxy - czx) + sq(axy - cyz) + sq(azx - byz)
    mixed = sq(ayz + bzx) + sq(ayz + cxy) + sq(bzx + cxy)
    high_order = sq(axyz) + sq(bxyz) + sq(cxyz)
    return (
        (lam / 16.0) * div
        + (2.0 * shear / 16.0) * diag
        + (shear / 16.0) * skew
        + ((lam + 1.5 * shear) / 48.0) * even
        + (1.5 * shear / 48.0) * odd
        + (shear / 48.0) * mixed
        + ((lam + 4.0 * shear) / 144.0) * high_order
    )


def smooth(windows, cols):
    lanes = lax.broadcasted_iota(jnp.int32, windows[0][0].shape, 1)
    total = None
    for dx in range(3):
        part = add_up(
            [weight(i, j, dx) * windows[i][j] for i in range(3) for j in range(3) if weight(i, j, dx) > 0.0]
        )
        if dx > 0:
            right = jnp.where(lanes < cols - dx, pltpu.roll(part, cols - dx, 1), 0.0)
            left = jnp.where(lanes >= dx, pltpu.roll(part, dx, 1), 0.0)
            part = left + right
        total = part if total is None else total + part
    return total


def row_sums(field, plane):
    at = lambda first: field[plane, first : first + 8, :]
    return [at(8), at(7) + at(9), at(6) + at(10)]


def z_sums(rows, plane):
    return [
        rows[plane],
        [a + b for a, b in zip(rows[plane - 1], rows[plane + 1])],
        [a + b for a, b in zip(rows[plane - 2], rows[plane + 2])],
    ]


def make_kernel(groups, slabs, slots, planes, rows, cols, tile):
    half = slots // 2
    chips = groups // 2
    below = planes + 1

    def kernel(
        disp, slot_node, node_weight, node_stiffness, design, out,
        field, low_face, high_face, sums, sibling, pair, arrived,
        des_edge, des_z, des_y, des_c, fac, fac_low,
        sen, sen_edge, sen_low, sen_high, sen_y, sen_cl, sen_ch, pad,
        load_sem, send_sem, recv_sem,
    ):
        group = lax.axis_index("nodes")
        slab = lax.axis_index("space")
        core = lax.rem(group, 2)
        chip = lax.div(group, 2)
        down = lax.rem(slab + slabs - 1, slabs)
        up = lax.rem(slab + 1, slabs)
        has_prev, has_next = group > 0, group < groups - 1
        slab_low = jnp.where(slab > 0, 1.0, 0.0).astype(jnp.float32)
        slab_high = jnp.where(slab < slabs - 1, 1.0, 0.0).astype(jnp.float32)
        mate = (group + 1 - 2 * core, slab)
        peers = [(2 * lax.rem(chip + k, chips) + core, slab) for k in range(1, chips)]

        def when(condition, action):
            if condition is None:
                action()
            else:
                pl.when(condition)(action)

        aside = group + 2 * core - 1
        partners = [(mate, None), ((group, down), None), ((group, up), None)]
        partners += [(peer, None) for peer in peers]
        partners.append(((aside, slab), (aside >= 0) & (aside < groups)))
        for cond, step in ((has_prev, -1), (has_next, 1)):
            partners += [((group + step, where), cond) for where in (down, up)]
        barrier = pltpu.get_barrier_semaphore()
        for device, cond in partners:
            when(cond, lambda: pl.semaphore_signal(barrier, inc=1, device_id=device, device_id_type=MESH))

        loads = []
        for slot in range(slots):
            load = pltpu.make_async_copy(
                disp.at[slot], field.at[slot, :, :, pl.ds(0, rows), :], load_sem.at[slot]
            )
            load.start()
            loads.append(load)
        zero_rows = jnp.zeros((8, cols), jnp.float32)
        for comp in range(3):
            for slot in range(slots):
                for plane in range(planes):
                    field[slot, comp, plane, rows : rows + 8, :] = zero_rows
            for slot in range(half):
                low_face[slot, comp, rows : rows + 8, :] = zero_rows
                high_face[slot, comp, rows : rows + 8, :] = zero_rows
        des_edge[0] = design[:, 0:2, :]
        des_edge[1] = design[:, tile - 2 : tile, :]

        pl.semaphore_wait(barrier, sum(1 if cond is None else cond.astype(jnp.int32) for _, cond in partners))

        count = [0]

        def remote(src, dst, device):
            number = count[0]
            count[0] += 1
            return pltpu.make_async_remote_copy(
                src_ref=src, dst_ref=dst, send_sem=send_sem.at[number], recv_sem=recv_sem.at[number],
                device_id=device, device_id_type=MESH,
            )

        def halo(edge, z_src, z_dst, y_dst, c_dst):
            copies = []
            for side, where in ((0, down), (1, up)):
                copies.append((remote(z_src[side], z_dst[side], (group, where)), None, None))
            for rim, (step, send_if, recv_if) in enumerate(((-1, has_prev, has_next), (1, has_next, has_prev))):
                copies.append((remote(edge.at[rim], y_dst.at[rim], (group + step, slab)), send_if, recv_if))
                for side, where in ((0, down), (1, up)):
                    part = edge.at[rim, pl.ds(*((0, edge.shape[1] - 2) if side == 0 else (edge.shape[1] - 2, 2)))]
                    copies.append((remote(part, c_dst[side].at[rim], (group + step, where)), send_if, recv_if))
            return copies

        def start_all(copies):
            for copy, send_if, _ in copies:
                when(send_if, copy.start)

        def wait_all(copies):
            for copy, send_if, recv_if in copies:
                when(recv_if, copy.wait_recv)
                when(send_if, copy.wait_send)

        design_halo = halo(
            des_edge,
            (design.at[pl.ds(0, 2)], design.at[pl.ds(planes - 2, 2)]),
            (des_z.at[1], des_z.at[0]),
            des_y,
            (des_c.at[1], des_c.at[0]),
        )
        start_all(design_halo)
        to_down, to_up = [], []
        for slot in range(half):
            to_down.append(
                remote(disp.at[slot, :, 0], high_face.at[slot, :, pl.ds(0, rows), :], (group, down))
            )
            to_down[-1].start()
            to_up.append(
                remote(
                    disp.at[half + slot, :, planes - 1], low_face.at[slot, :, pl.ds(0, rows), :], (group, up)
                )
            )
            to_up[-1].start()

        coef = []
        for slot in range(slots):
            node = slot_node[slot]
            index = jnp.clip(node, 0, node_weight.shape[0] - 1)
            value = node_weight[index] * node_stiffness[index]
            coef.append(jnp.where(node < node_weight.shape[0], value, 0.0))

        last = lax.broadcasted_iota(jnp.int32, (8, cols), 1) == cols - 1
        next_rows = lax.broadcasted_iota(jnp.int32, (8, cols), 0) == 0

        def modes_of(plane_ref, block, gain=None):
            def load(comp):
                pair_of = [
                    plane_ref[comp, pl.ds(pl.multiple_of((block + k) * 8, 8), 8), :] for k in range(2)
                ]
                return pair_of if gain is None else [v * gain for v in pair_of]

            return plane_modes(load, next_rows, last)

        for slot in range(slots):
            loads[slot].wait()

            def block_step(block, carry):
                here = modes_of(field.at[slot, :, 0], block)
                for layer in range(planes - 1):
                    above = modes_of(field.at[slot, :, layer + 1], block)
                    value = coef[slot] * layer_energy(here, above)
                    place = (lax.rem(block, 2), lax.div(block, 2), layer + 1)
                    sums[place] = value if slot == 0 else sums[place] + value
                    here = above
                return carry

            lax.fori_loop(0, rows // 8, block_step, 0)

        wait_all(design_halo)
        pad[pl.ds(2, planes), pl.ds(8, tile), :] = design[...]
        pad[pl.ds(0, 2), pl.ds(8, tile), :] = des_z[0] * slab_low
        pad[pl.ds(planes + 2, 2), pl.ds(8, tile), :] = des_z[1] * slab_high
        for rim, (first, cond) in enumerate(((16, has_next), (6, has_prev))):
            inside = lambda v: jnp.where(cond, v, 0.0)
            pad[pl.ds(2, planes), pl.ds(first, 2), :] = inside(des_y[rim])
            pad[pl.ds(0, 2), pl.ds(first, 2), :] = inside(des_c[0, rim]) * slab_low
            pad[pl.ds(planes + 2, 2), pl.ds(first, 2), :] = inside(des_c[1, rim]) * slab_high

        row_at = lax.broadcasted_iota(jnp.int32, (tile, cols), 0) + group * tile
        ones = []
        for dy in range(3):
            within = lambda y: jnp.where((y >= 0) & (y < groups * tile), 1.0, 0.0)
            ones.append(within(row_at) if dy == 0 else within(row_at - dy) + within(row_at + dy))
        base = math.tanh(BETA * ETA)
        scale = base + math.tanh(BETA * (1.0 - ETA))
        filt_rows = [row_sums(pad, p) for p in range(planes + 4)]
        for plane in range(planes):
            z = slab * planes + plane
            here = lambda d: jnp.where((z + d >= 0) & (z + d < slabs * planes), 1.0, 0.0)
            gains = [1.0, here(-1) + here(1), here(-2) + here(2)]
            cover = smooth([[v * gain for v in ones] for gain in gains], cols)
            filtered = smooth(z_sums(filt_rows, plane + 2), cols) / cover
            level = jnp.tanh(BETA * (filtered - ETA))
            projected = (base + level) / scale
            slope = BETA * (1.0 - level * level) / scale
            fac[plane] = (-3.0 * (1.0 - E_FLOOR)) * (projected * projected) * slope / cover
        factor_up = remote(fac.at[planes - 1], fac_low, (group, up))
        factor_up.start()

        for slot in range(half):
            to_up[slot].wait_recv()
            to_down[slot].wait_recv()

            def face_step(block, carry):
                place = lambda layer: (lax.rem(block, 2), lax.div(block, 2), layer)
                lower = layer_energy(
                    modes_of(low_face.at[slot], block),
                    modes_of(field.at[half + slot, :, 0], block, slab_low),
                )
                value = coef[half + slot] * lower
                sums[place(0)] = value if slot == 0 else sums[place(0)] + value
                upper = layer_energy(
                    modes_of(field.at[slot, :, planes - 1], block),
                    modes_of(high_face.at[slot], block, slab_high),
                )
                value = coef[slot] * upper
                sums[place(planes)] = value if slot == 0 else sums[place(planes)] + value
                return carry

            lax.fori_loop(0, rows // 8, face_step, 0)

        swap = remote(sums.at[1 - core], sibling, mate)
        swap.start()
        swap.wait_recv()
        for index in range(chips):
            pair[index] = sums[core, index] + sibling[index]
        spread = []
        for k in range(1, chips):
            spread.append(remote(pair.at[lax.rem(chip + k, chips)], arrived.at[k - 1], peers[k - 1]))
            spread[-1].start()
        factor_up.wait_recv()
        for copy in spread:
            copy.wait_recv()
        for plane in range(below):
            total = pair[chip, plane] + add_up([arrived[k, plane] for k in range(chips - 1)])
            sen[plane] = total * (fac_low[...] if plane == 0 else fac[plane - 1])
        sen_edge[0] = sen[:, 0:2, :]
        sen_edge[1] = sen[:, tile - 2 : tile, :]

        sens_halo = halo(
            sen_edge,
            (sen.at[pl.ds(0, 3)], sen.at[pl.ds(below - 2, 2)]),
            (sen_high, sen_low),
            sen_y,
            (sen_ch, sen_cl),
        )
        start_all(sens_halo)
        wait_all(sens_halo)

        def place_rows(first, own, lower, upper):
            span = pl.ds(first, own.shape[1])
            pad[0, span, :] = lower[0] * slab_low
            pad[1, span, :] = (lower[1] + own[0]) * slab_low
            for plane in range(planes - 1):
                pad[2 + plane, span, :] = own[1 + plane]
            pad[1 + planes, span, :] = own[planes] + upper[0]
            pad[2 + planes, span, :] = upper[1] * slab_high
            pad[3 + planes, span, :] = upper[2] * slab_high

        place_rows(8, sen[...], sen_low[...], sen_high[...])
        for rim, (first, cond) in enumerate(((16, has_next), (6, has_prev))):
            inside = lambda v: jnp.where(cond, v, 0.0)
            place_rows(first, inside(sen_y[rim]), inside(sen_cl[rim]), inside(sen_ch[rim]))
        sens_rows = [row_sums(pad, p) for p in range(planes + 4)]
        for plane in range(planes):
            out[plane] = smooth(z_sums(sens_rows, plane + 2), cols)

        swap.wait_send()
        factor_up.wait_send()
        for copy in spread + to_up + to_down:
            copy.wait_send()

    vmem = lambda *shape: pltpu.VMEM(shape, jnp.float32)
    copies = 8 + 2 * half + 1 + 1 + (chips - 1) + 8
    scratch = [
        vmem(slots, 3, planes, rows + 8, cols),
        vmem(half, 3, rows + 8, cols),
        vmem(half, 3, rows + 8, cols),
        vmem(2, chips, below, tile, cols),
        vmem(chips, below, tile, cols),
        vmem(chips, below, tile, cols),
        vmem(chips - 1, below, tile, cols),
        vmem(2, planes, 2, cols),
        vmem(2, 2, tile, cols),
        vmem(2, planes, 2, cols),
        vmem(2, 2, 2, 2, cols),
        vmem(planes, tile, cols),
        vmem(tile, cols),
        vmem(below, tile, cols),
        vmem(2, below, 2, cols),
        vmem(2, tile, cols),
        vmem(3, tile, cols),
        vmem(2, below, 2, cols),
        vmem(2, 2, 2, cols),
        vmem(2, 3, 2, cols),
        vmem(planes + 4, 24, cols),
        pltpu.SemaphoreType.DMA((slots,)),
        pltpu.SemaphoreType.DMA((copies,)),
        pltpu.SemaphoreType.DMA((copies,)),
    ]
    return kernel, scratch


def solution(mesh):
    groups, slabs = mesh.shape["nodes"], mesh.shape["space"]

    def per_device(displacement, slot_node, node_weight, node_stiffness, design):
        slots, _, planes, rows, cols = displacement.shape
        kernel, scratch = make_kernel(groups, slabs, slots, planes, rows, cols, design.shape[1])
        smem = pl.BlockSpec(memory_space=pltpu.SMEM)
        vmem = pl.BlockSpec(memory_space=pltpu.VMEM)
        return pl.pallas_call(
            kernel,
            out_shape=jax.ShapeDtypeStruct(design.shape, jnp.float32),
            in_specs=[pl.BlockSpec(memory_space=pl.ANY), smem, smem, smem, vmem],
            out_specs=vmem,
            scratch_shapes=scratch,
            compiler_params=pltpu.CompilerParams(
                collective_id=0, has_side_effects=True, vmem_limit_bytes=48 * 2**20
            ),
            cost_estimate=pl.CostEstimate(flops=40_000_000, bytes_accessed=4_000_000, transcendentals=8192),
            name="sensitivity",
        )(displacement, slot_node, node_weight, node_stiffness, design)

    return jax.shard_map(
        per_device,
        mesh=mesh,
        in_specs=(
            P("nodes", None, "space", None, None),
            P("nodes"),
            P(),
            P(),
            P("space", "nodes", None),
        ),
        out_specs=P("space", "nodes", None),
        check_vma=False,
    )
```

```python
import math

import jax
import jax.numpy as jnp
from jax import lax
from jax.experimental import pallas as pl
from jax.experimental.pallas import tpu as pltpu
from jax.sharding import PartitionSpec as P

POISSON = 0.3
E_FLOOR = 0.001
BETA = 8.0
ETA = 0.5
RADIUS = 2.5
MESH = pl.DeviceIdType.MESH
RUN = 4
RELAY_DOWN = {1: (3, 0), 4: (3, 1), 2: (1, 0), 5: (2, 0)}
RELAY_UP = {1: (0, 0), 4: (0, 1), 2: (2, 1), 5: (1, 1)}


def weight(dz, dy, dx):
    return max(0.0, RADIUS - math.sqrt(dz * dz + dy * dy + dx * dx))


def add_up(terms):
    total = None
    for term in terms:
        total = term if total is None else total + term
    return total


def next_lane(v, last):
    return jnp.where(last, 0.0, pltpu.roll(v, v.shape[1] - 1, 1))


def plane_modes(load, next_rows, last):
    modes = []
    for comp in range(3):
        here, below = load(comp)
        up = pltpu.roll(jnp.where(next_rows, below, here), 7, 0)
        ysum, ydif = up + here, up - here
        ysum_x, ydif_x = next_lane(ysum, last), next_lane(ydif, last)
        modes.append((ysum_x + ysum, ysum_x - ysum, ydif_x + ydif, ydif_x - ydif))
    return modes


def layer_energy(low, high):
    lam = POISSON / ((1.0 + POISSON) * (1.0 - 2.0 * POISSON))
    shear = 1.0 / (2.0 * (1.0 + POISSON))
    sums = [[lo + hi for lo, hi in zip(a, b)] for a, b in zip(low, high)]
    difs = [[hi - lo for lo, hi in zip(a, b)] for a, b in zip(low, high)]
    (_, ax, ay, axy), (_, bx, by, bxy), (_, cx, cy, cxy) = sums
    (az, azx, ayz, axyz), (bz, bzx, byz, bxyz), (cz, czx, cyz, cxyz) = difs
    sq = lambda v: v * v
    div = sq(ax + by + cz)
    diag = sq(ax) + sq(by) + sq(cz)
    skew = sq(ay + bx) + sq(az + cx) + sq(bz + cy)
    even = sq(bxy + czx) + sq(axy + cyz) + sq(azx + byz)
    odd = sq(bxy - czx) + sq(axy - cyz) + sq(azx - byz)
    mixed = sq(ayz + bzx) + sq(ayz + cxy) + sq(bzx + cxy)
    high_order = sq(axyz) + sq(bxyz) + sq(cxyz)
    return (
        (lam / 16.0) * div
        + (2.0 * shear / 16.0) * diag
        + (shear / 16.0) * skew
        + ((lam + 1.5 * shear) / 48.0) * even
        + (1.5 * shear / 48.0) * odd
        + (shear / 48.0) * mixed
        + ((lam + 4.0 * shear) / 144.0) * high_order
    )


def smooth(windows, cols):
    lanes = lax.broadcasted_iota(jnp.int32, windows[0][0].shape, 1)
    total = None
    for dx in range(3):
        part = add_up(
            [weight(i, j, dx) * windows[i][j] for i in range(3) for j in range(3) if weight(i, j, dx) > 0.0]
        )
        if dx > 0:
            right = jnp.where(lanes < cols - dx, pltpu.roll(part, cols - dx, 1), 0.0)
            left = jnp.where(lanes >= dx, pltpu.roll(part, dx, 1), 0.0)
            part = left + right
        total = part if total is None else total + part
    return total


def row_sums(field, plane):
    at = lambda first: field[plane, first : first + 8, :]
    return [at(8), at(7) + at(9), at(6) + at(10)]


def z_sums(rows, plane):
    return [
        rows[plane],
        [a + b for a, b in zip(rows[plane - 1], rows[plane + 1])],
        [a + b for a, b in zip(rows[plane - 2], rows[plane + 2])],
    ]


def make_kernel(groups, slabs, nodes, slots, planes, rows, cols, tile):
    half = slots // 2
    chips = groups // 2
    below = planes + 1

    def kernel(
        disp, slot_node_in, node_weight_in, node_stiffness_in, design_in, out,
        slot_node, node_weight, node_stiffness, design, field, low_face, high_face, sums, sibling, pair, arrived,
        des_edge, des_z, des_y, des_c, fac, fac_low,
        sen, sen_edge, sen_low, sen_high, sen_y, sen_cl, sen_ch, pad,
        relay, load_sem, small_sem, send_sem, recv_sem, face_send, face_recv, relay_send, relay_recv,
    ):
        group = lax.axis_index("nodes")
        slab = lax.axis_index("space")
        core = lax.rem(group, 2)
        chip = lax.div(group, 2)
        place = lax.rem(slab, RUN)
        run = slab - place
        down, up = slab - 1, slab + 1
        has_prev, has_next = group > 0, group < groups - 1
        has_down, has_up = slab > 0, slab < slabs - 1
        run_down, run_up = run > 0, run < slabs - RUN
        mate = (group + 1 - 2 * core, slab)
        peers = [(2 * lax.rem(chip + k, chips) + core, slab) for k in range(1, chips)]

        def when(condition, action):
            if condition is None:
                action()
            else:
                pl.when(condition)(action)

        small = []
        for number, (source, target) in enumerate(
            (
                (design_in, design),
                (slot_node_in, slot_node),
                (node_weight_in, node_weight),
                (node_stiffness_in, node_stiffness),
            )
        ):
            small.append(pltpu.make_async_copy(source, target, small_sem.at[number]))
            small[-1].start()

        aside = group + 2 * core - 1
        partners = [(mate, None)] + [(peer, None) for peer in peers]
        partners.append(((aside, slab), (aside >= 0) & (aside < groups)))
        partners += [((group, run + lax.rem(place + k, RUN)), None) for k in range(1, RUN)]
        partners += [((group, run - 1), run_down), ((group, run + RUN), run_up)]
        for k in range(1, RUN):
            partners.append(((group, slab - 1 - k), run_down & (place == 0)))
            partners.append(((group, slab + 1 + k), run_up & (place == RUN - 1)))
        for cond, step in ((has_prev, -1), (has_next, 1)):
            partners += [((group + step, down), cond & has_down), ((group + step, up), cond & has_up)]
        barrier = pltpu.get_barrier_semaphore()
        for device, cond in partners:
            when(cond, lambda: pl.semaphore_signal(barrier, inc=1, device_id=device, device_id_type=MESH))

        loads = []
        for slot in range(slots):
            load = pltpu.make_async_copy(
                disp.at[slot], field.at[slot, :, :, pl.ds(0, rows), :], load_sem.at[slot]
            )
            load.start()
            loads.append(load)
        zero_rows = jnp.zeros((8, cols), jnp.float32)
        for comp in range(3):
            for slot in range(slots):
                for plane in range(planes):
                    field[slot, comp, plane, rows : rows + 8, :] = zero_rows
            for slot in range(half):
                low_face[slot, comp, rows : rows + 8, :] = zero_rows
                high_face[slot, comp, rows : rows + 8, :] = zero_rows

        def clear(face_ref):
            for slot in range(half):
                for comp in range(3):
                    face_ref[slot, comp, 0:rows, :] = jnp.zeros((rows, cols), jnp.float32)

        pl.when(slab == 0)(lambda: clear(low_face))
        pl.when(slab == slabs - 1)(lambda: clear(high_face))
        small[0].wait()
        des_edge[0] = design[:, 0:2, :]
        des_edge[1] = design[:, tile - 2 : tile, :]

        pl.semaphore_wait(barrier, sum(1 if cond is None else cond.astype(jnp.int32) for _, cond in partners))

        count = [0]

        def remote(src, dst, device):
            number = count[0]
            count[0] += 1
            return pltpu.make_async_remote_copy(
                src_ref=src, dst_ref=dst, send_sem=send_sem.at[number], recv_sem=recv_sem.at[number],
                device_id=device, device_id_type=MESH,
            )

        def halo(edge, z_src, z_dst, y_dst, c_dst):
            copies = []
            ways = ((0, down, has_down, has_up), (1, up, has_up, has_down))
            for side, where, send_z, recv_z in ways:
                copies.append((remote(z_src[side], z_dst[side], (group, where)), send_z, recv_z))
            for rim, (step, send_if, recv_if) in enumerate(((-1, has_prev, has_next), (1, has_next, has_prev))):
                copies.append((remote(edge.at[rim], y_dst.at[rim], (group + step, slab)), send_if, recv_if))
                for side, where, send_z, recv_z in ways:
                    part = edge.at[rim, pl.ds(*((0, edge.shape[1] - 2) if side == 0 else (edge.shape[1] - 2, 2)))]
                    copy = remote(part, c_dst[side].at[rim], (group + step, where))
                    copies.append((copy, send_if & send_z, recv_if & recv_z))
            return copies

        def start_all(copies):
            for copy, send_if, _ in copies:
                when(send_if, copy.start)

        def wait_all(copies):
            for copy, send_if, recv_if in copies:
                when(recv_if, copy.wait_recv)
                when(send_if, copy.wait_send)

        face_of = lambda faces, plane: faces.at[plane // 3, plane % 3, pl.ds(0, rows), :]

        def face_copy(way, plane, where, stop=None, source=None, sent=None):
            if source is None:
                source = (
                    disp.at[plane // 3, plane % 3, 0]
                    if way == 0
                    else disp.at[half + plane // 3, plane % 3, planes - 1]
                )
            return pltpu.make_async_remote_copy(
                src_ref=source,
                dst_ref=face_of((high_face, low_face)[way], plane) if stop is None else relay.at[stop],
                send_sem=face_send.at[way, plane] if sent is None else sent,
                recv_sem=face_recv.at[way, plane] if stop is None else relay_recv.at[stop],
                device_id=(group, where),
                device_id_type=MESH,
            )

        ways = (
            (0, down, has_down, has_up, RELAY_DOWN, 0, run_down, run - 1),
            (1, up, has_up, has_down, RELAY_UP, RUN - 1, run_up, run + RUN),
        )
        for plane in (1, 2, 5, 4, 0, 3):
            for way, where, send_if, _, relays, end, crosses, _ in ways:
                if plane in relays:
                    at, stop = relays[plane]
                    pl.when(crosses & (place == end))(face_copy(way, plane, run + at, stop).start)
                    pl.when(place != end)(face_copy(way, plane, where).start)
                else:
                    pl.when(send_if)(face_copy(way, plane, where).start)

        def pass_on(stop):
            for way, _, _, _, relays, _, crosses, target in ways:
                for plane, (at, slot) in relays.items():
                    if slot == stop:

                        def forward():
                            copy = face_copy(way, plane, target, source=relay.at[stop], sent=relay_send.at[stop])
                            face_copy(way, plane, target, stop).wait_recv()
                            copy.start()

                        pl.when(crosses & (place == at))(forward)

        design_halo = halo(
            des_edge,
            (design.at[pl.ds(0, 2)], design.at[pl.ds(planes - 2, 2)]),
            (des_z.at[1], des_z.at[0]),
            des_y,
            (des_c.at[1], des_c.at[0]),
        )
        start_all(design_halo)
        for copy in small[1:]:
            copy.wait()

        coef = []
        for slot in range(slots):
            node = slot_node[slot]
            index = jnp.clip(node, 0, node_weight.shape[0] - 1)
            value = node_weight[index] * node_stiffness[index]
            coef.append(jnp.where(node < node_weight.shape[0], value, 0.0))

        last = lax.broadcasted_iota(jnp.int32, (8, cols), 1) == cols - 1
        next_rows = lax.broadcasted_iota(jnp.int32, (8, cols), 0) == 0

        def modes_of(plane_ref, block):
            def load(comp):
                return [plane_ref[comp, pl.ds(pl.multiple_of((block + k) * 8, 8), 8), :] for k in range(2)]

            return plane_modes(load, next_rows, last)

        for slot in range(slots):
            loads[slot].wait()

            def block_step(block, carry):
                here = modes_of(field.at[slot, :, 0], block)
                for layer in range(planes - 1):
                    above = modes_of(field.at[slot, :, layer + 1], block)
                    value = coef[slot] * layer_energy(here, above)
                    where = (lax.rem(block, 2), lax.div(block, 2), layer + 1)
                    sums[where] = value if slot == 0 else sums[where] + value
                    here = above
                return carry

            lax.fori_loop(0, rows // 8, block_step, 0)
            if slot < 2:
                pass_on(slot)

        wait_all(design_halo)
        pad[pl.ds(2, planes), pl.ds(8, tile), :] = design[...]
        pad[pl.ds(0, 2), pl.ds(8, tile), :] = jnp.where(has_down, des_z[0], 0.0)
        pad[pl.ds(planes + 2, 2), pl.ds(8, tile), :] = jnp.where(has_up, des_z[1], 0.0)
        for rim, (first, cond) in enumerate(((16, has_next), (6, has_prev))):
            pad[pl.ds(2, planes), pl.ds(first, 2), :] = jnp.where(cond, des_y[rim], 0.0)
            pad[pl.ds(0, 2), pl.ds(first, 2), :] = jnp.where(cond & has_down, des_c[0, rim], 0.0)
            pad[pl.ds(planes + 2, 2), pl.ds(first, 2), :] = jnp.where(cond & has_up, des_c[1, rim], 0.0)

        row_at = lax.broadcasted_iota(jnp.int32, (tile, cols), 0) + group * tile
        ones = []
        for dy in range(3):
            within = lambda y: jnp.where((y >= 0) & (y < groups * tile), 1.0, 0.0)
            ones.append(within(row_at) if dy == 0 else within(row_at - dy) + within(row_at + dy))
        base = math.tanh(BETA * ETA)
        scale = base + math.tanh(BETA * (1.0 - ETA))
        filt_rows = [row_sums(pad, p) for p in range(planes + 4)]
        for plane in range(planes):
            z = slab * planes + plane
            here = lambda d: jnp.where((z + d >= 0) & (z + d < slabs * planes), 1.0, 0.0)
            gains = [1.0, here(-1) + here(1), here(-2) + here(2)]
            cover = smooth([[v * gain for v in ones] for gain in gains], cols)
            filtered = smooth(z_sums(filt_rows, plane + 2), cols) / cover
            level = jnp.tanh(BETA * (filtered - ETA))
            projected = (base + level) / scale
            slope = BETA * (1.0 - level * level) / scale
            fac[plane] = (-3.0 * (1.0 - E_FLOOR)) * (projected * projected) * slope / cover
        factor_up = remote(fac.at[planes - 1], fac_low, (group, up))
        pl.when(has_up)(factor_up.start)

        for slot in range(half):
            for comp in range(3):
                for way, where, _, recv_if, *_ in ways:
                    pl.when(recv_if)(face_copy(way, 3 * slot + comp, where).wait_recv)

            def face_step(block, carry):
                spot = lambda layer: (lax.rem(block, 2), lax.div(block, 2), layer)
                lower = layer_energy(
                    modes_of(low_face.at[slot], block), modes_of(field.at[half + slot, :, 0], block)
                )
                value = coef[half + slot] * lower
                sums[spot(0)] = value if slot == 0 else sums[spot(0)] + value
                upper = layer_energy(
                    modes_of(field.at[slot, :, planes - 1], block), modes_of(high_face.at[slot], block)
                )
                value = coef[slot] * upper
                sums[spot(planes)] = value if slot == 0 else sums[spot(planes)] + value
                return carry

            lax.fori_loop(0, rows // 8, face_step, 0)

        def top():
            def top_step(block, carry):
                spot = (lax.rem(block, 2), lax.div(block, 2), planes)
                zero = jnp.zeros((8, cols), jnp.float32)
                for slot in range(half, slots):
                    modes = modes_of(field.at[slot, :, planes - 1], block)
                    sums[spot] += coef[slot] * layer_energy(modes, [(zero,) * 4] * 3)
                return carry

            lax.fori_loop(0, rows // 8, top_step, 0)

        pl.when(slab == slabs - 1)(top)

        swap = remote(sums.at[1 - core], sibling, mate)
        swap.start()
        swap.wait_recv()
        for index in range(chips):
            pair[index] = sums[core, index] + sibling[index]
        spread = []
        for k in range(1, chips):
            spread.append(remote(pair.at[lax.rem(chip + k, chips)], arrived.at[k - 1], peers[k - 1]))
            spread[-1].start()
        pl.when(has_down)(factor_up.wait_recv)
        for copy in spread:
            copy.wait_recv()
        for plane in range(below):
            total = pair[chip, plane] + add_up([arrived[k, plane] for k in range(chips - 1)])
            sen[plane] = total * (jnp.where(has_down, fac_low[...], 0.0) if plane == 0 else fac[plane - 1])
        sen_edge[0] = sen[:, 0:2, :]
        sen_edge[1] = sen[:, tile - 2 : tile, :]

        sens_halo = halo(
            sen_edge,
            (sen.at[pl.ds(0, 3)], sen.at[pl.ds(below - 2, 2)]),
            (sen_high, sen_low),
            sen_y,
            (sen_ch, sen_cl),
        )
        start_all(sens_halo)
        wait_all(sens_halo)

        def place_rows(first, cond, own, lower, upper):
            span = pl.ds(first, own.shape[1])
            inside = lambda flag, v: v if flag is None else jnp.where(flag, v, 0.0)
            both = lambda flag: flag if cond is None else cond & flag
            pad[0, span, :] = inside(both(has_down), lower[0])
            pad[1, span, :] = inside(both(has_down), lower[1] + own[0])
            for plane in range(planes - 1):
                pad[2 + plane, span, :] = inside(cond, own[1 + plane])
            pad[1 + planes, span, :] = inside(cond, own[planes]) + inside(both(has_up), upper[0])
            pad[2 + planes, span, :] = inside(both(has_up), upper[1])
            pad[3 + planes, span, :] = inside(both(has_up), upper[2])

        place_rows(8, None, sen, sen_low, sen_high)
        for rim, (first, cond) in enumerate(((16, has_next), (6, has_prev))):
            place_rows(first, cond, sen_y.at[rim], sen_cl.at[rim], sen_ch.at[rim])
        sens_rows = [row_sums(pad, p) for p in range(planes + 4)]
        for plane in range(planes):
            out[plane] = smooth(z_sums(sens_rows, plane + 2), cols)

        swap.wait_send()
        pl.when(has_up)(factor_up.wait_send)
        for copy in spread:
            copy.wait_send()
        for plane in range(3 * half):
            for way, where, send_if, *_ in ways:
                pl.when(send_if)(face_copy(way, plane, where).wait_send)
        for way, where, _, _, relays, _, crosses, _ in ways:
            for plane, (at, stop) in relays.items():
                copy = face_copy(way, plane, where, source=relay.at[stop], sent=relay_send.at[stop])
                pl.when(crosses & (place == at))(copy.wait_send)

    vmem = lambda *shape: pltpu.VMEM(shape, jnp.float32)
    copies = 8 + 1 + 1 + (chips - 1) + 8
    scratch = [
        pltpu.SMEM((slots,), jnp.int32),
        pltpu.SMEM((nodes,), jnp.float32),
        pltpu.SMEM((nodes,), jnp.float32),
        vmem(planes, tile, cols),
        vmem(slots, 3, planes, rows + 8, cols),
        vmem(half, 3, rows + 8, cols),
        vmem(half, 3, rows + 8, cols),
        vmem(2, chips, below, tile, cols),
        vmem(chips, below, tile, cols),
        vmem(chips, below, tile, cols),
        vmem(chips - 1, below, tile, cols),
        vmem(2, planes, 2, cols),
        vmem(2, 2, tile, cols),
        vmem(2, planes, 2, cols),
        vmem(2, 2, 2, 2, cols),
        vmem(planes, tile, cols),
        vmem(tile, cols),
        vmem(below, tile, cols),
        vmem(2, below, 2, cols),
        vmem(2, tile, cols),
        vmem(3, tile, cols),
        vmem(2, below, 2, cols),
        vmem(2, 2, 2, cols),
        vmem(2, 3, 2, cols),
        vmem(planes + 4, 24, cols),
        vmem(2, rows, cols),
        pltpu.SemaphoreType.DMA((slots,)),
        pltpu.SemaphoreType.DMA((4,)),
        pltpu.SemaphoreType.DMA((copies,)),
        pltpu.SemaphoreType.DMA((copies,)),
        pltpu.SemaphoreType.DMA((2, 3 * half)),
        pltpu.SemaphoreType.DMA((2, 3 * half)),
        pltpu.SemaphoreType.DMA((2,)),
        pltpu.SemaphoreType.DMA((2,)),
    ]
    return kernel, scratch


def solution(mesh):
    groups, slabs = mesh.shape["nodes"], mesh.shape["space"]

    def per_device(displacement, slot_node, node_weight, node_stiffness, design):
        slots, _, planes, rows, cols = displacement.shape
        kernel, scratch = make_kernel(groups, slabs, node_weight.shape[0], slots, planes, rows, cols, design.shape[1])
        return pl.pallas_call(
            kernel,
            out_shape=jax.ShapeDtypeStruct(design.shape, jnp.float32),
            in_specs=[pl.BlockSpec(memory_space=pltpu.HBM)] * 5,
            out_specs=pl.BlockSpec(memory_space=pltpu.VMEM),
            scratch_shapes=scratch,
            compiler_params=pltpu.CompilerParams(
                collective_id=0, has_side_effects=True, vmem_limit_bytes=60 * 2**20
            ),
            cost_estimate=pl.CostEstimate(flops=40_000_000, bytes_accessed=4_000_000, transcendentals=8192),
            name="sensitivity",
        )(displacement, slot_node, node_weight, node_stiffness, design)

    return jax.shard_map(
        per_device,
        mesh=mesh,
        in_specs=(
            P("nodes", None, "space", None, None),
            P("nodes"),
            P(),
            P(),
            P("space", "nodes", None),
        ),
        out_specs=P("space", "nodes", None),
        check_vma=False,
    )
```

```python
import math

import jax
import jax.numpy as jnp
from jax import lax
from jax.experimental import pallas as pl
from jax.experimental.pallas import tpu as pltpu
from jax.sharding import PartitionSpec as P

POISSON = 0.3
E_FLOOR = 0.001
BETA = 8.0
ETA = 0.5
RADIUS = 2.5
MESH = pl.DeviceIdType.MESH
RUN = 4
RELAY_DOWN = {1: (3, 0), 4: (3, 1), 2: (1, 0), 5: (2, 0)}
RELAY_UP = {1: (0, 0), 4: (0, 1), 2: (2, 1), 5: (1, 1)}


def weight(dz, dy, dx):
    return max(0.0, RADIUS - math.sqrt(dz * dz + dy * dy + dx * dx))


def add_up(terms):
    total = None
    for term in terms:
        total = term if total is None else total + term
    return total


def next_lane(v, last):
    return jnp.where(last, 0.0, pltpu.roll(v, v.shape[1] - 1, 1))


def plane_modes(load, next_rows, last):
    modes = []
    for comp in range(3):
        here, below = load(comp)
        up = pltpu.roll(jnp.where(next_rows, below, here), 7, 0)
        ysum, ydif = up + here, up - here
        ysum_x, ydif_x = next_lane(ysum, last), next_lane(ydif, last)
        modes.append((ysum_x + ysum, ysum_x - ysum, ydif_x + ydif, ydif_x - ydif))
    return modes


def layer_energy(low, high):
    lam = POISSON / ((1.0 + POISSON) * (1.0 - 2.0 * POISSON))
    shear = 1.0 / (2.0 * (1.0 + POISSON))
    sums = [[lo + hi for lo, hi in zip(a, b)] for a, b in zip(low, high)]
    difs = [[hi - lo for lo, hi in zip(a, b)] for a, b in zip(low, high)]
    (_, ax, ay, axy), (_, bx, by, bxy), (_, cx, cy, cxy) = sums
    (az, azx, ayz, axyz), (bz, bzx, byz, bxyz), (cz, czx, cyz, cxyz) = difs
    sq = lambda v: v * v
    div = sq(ax + by + cz)
    diag = sq(ax) + sq(by) + sq(cz)
    skew = sq(ay + bx) + sq(az + cx) + sq(bz + cy)
    even = sq(bxy + czx) + sq(axy + cyz) + sq(azx + byz)
    odd = sq(bxy - czx) + sq(axy - cyz) + sq(azx - byz)
    mixed = sq(ayz + bzx) + sq(ayz + cxy) + sq(bzx + cxy)
    high_order = sq(axyz) + sq(bxyz) + sq(cxyz)
    return (
        (lam / 16.0) * div
        + (2.0 * shear / 16.0) * diag
        + (shear / 16.0) * skew
        + ((lam + 1.5 * shear) / 48.0) * even
        + (1.5 * shear / 48.0) * odd
        + (shear / 48.0) * mixed
        + ((lam + 4.0 * shear) / 144.0) * high_order
    )


def smooth(windows, cols):
    lanes = lax.broadcasted_iota(jnp.int32, windows[0][0].shape, 1)
    total = None
    for dx in range(3):
        part = add_up(
            [weight(i, j, dx) * windows[i][j] for i in range(3) for j in range(3) if weight(i, j, dx) > 0.0]
        )
        if dx > 0:
            right = jnp.where(lanes < cols - dx, pltpu.roll(part, cols - dx, 1), 0.0)
            left = jnp.where(lanes >= dx, pltpu.roll(part, dx, 1), 0.0)
            part = left + right
        total = part if total is None else total + part
    return total


def row_sums(field, plane):
    at = lambda first: field[plane, first : first + 8, :]
    return [at(8), at(7) + at(9), at(6) + at(10)]


def z_sums(rows, plane):
    return [
        rows[plane],
        [a + b for a, b in zip(rows[plane - 1], rows[plane + 1])],
        [a + b for a, b in zip(rows[plane - 2], rows[plane + 2])],
    ]


def make_kernel(groups, slabs, nodes, slots, planes, rows, cols, tile):
    half = slots // 2
    chips = groups // 2

    def kernel(
        disp, slot_node_in, node_weight_in, node_stiffness_in, design_in, out,
        slot_node, node_weight, node_stiffness, design, field, low_face, high_face, relay,
        des_pad, des_z, des_edge, des_y, fac, fac_low,
        in_sums, in_mate, in_pair, in_peers, sen, sen_pad, sen_low, sen_high, sen_cl, sen_ch, sen_edge, sen_y,
        face_sums, face_mate, face_pair, face_peers, late, late_z, late_c,
        load_sem, small_sem, send_sem, recv_sem, face_send, face_recv, relay_send, relay_recv,
    ):
        group = lax.axis_index("nodes")
        slab = lax.axis_index("space")
        core = lax.rem(group, 2)
        chip = lax.div(group, 2)
        place = lax.rem(slab, RUN)
        run = slab - place
        down, up = slab - 1, slab + 1
        has_prev, has_next = group > 0, group < groups - 1
        has_down, has_up = slab > 0, slab < slabs - 1
        run_down, run_up = run > 0, run < slabs - RUN
        mate = (group + 1 - 2 * core, slab)
        peers = [(2 * lax.rem(chip + k, chips) + core, slab) for k in range(1, chips)]

        def when(condition, action):
            if condition is None:
                action()
            else:
                pl.when(condition)(action)

        aside = group + 2 * core - 1
        partners = [(mate, None)] + [(peer, None) for peer in peers]
        partners.append(((aside, slab), (aside >= 0) & (aside < groups)))
        partners += [((group, run + lax.rem(place + k, RUN)), None) for k in range(1, RUN)]
        partners.append(((group, down), run_down & (place == 0)))
        partners.append(((group, up), run_up & (place == RUN - 1)))
        barrier = pltpu.get_barrier_semaphore()
        for device, cond in partners:
            when(cond, lambda: pl.semaphore_signal(barrier, inc=1, device_id=device, device_id_type=MESH))
        loads = []
        for slot in range(slots):
            load = pltpu.make_async_copy(
                disp.at[slot], field.at[slot, :, :, pl.ds(0, rows), :], load_sem.at[slot]
            )
            load.start()
            loads.append(load)
        small = []
        for number, (source, target) in enumerate(
            (
                (design_in, design),
                (slot_node_in, slot_node),
                (node_weight_in, node_weight),
                (node_stiffness_in, node_stiffness),
            )
        ):
            small.append(pltpu.make_async_copy(source, target, small_sem.at[number]))
            small[-1].start()
        pl.semaphore_wait(barrier, sum(1 if cond is None else cond.astype(jnp.int32) for _, cond in partners))

        started = []

        def remote(src, dst, device, send_if=None, recv_if=None):
            number = len(started)
            copy = pltpu.make_async_remote_copy(
                src_ref=src, dst_ref=dst, send_sem=send_sem.at[number], recv_sem=recv_sem.at[number],
                device_id=device, device_id_type=MESH,
            )
            started.append((copy, send_if, recv_if))
            when(send_if, copy.start)
            return started[-1:]

        def arrive(copies):
            for copy, _, recv_if in copies:
                when(recv_if, copy.wait_recv)

        def send_z(below_src, below_dst, above_src, above_dst):
            return remote(below_src, below_dst, (group, down), has_down, has_up) + remote(
                above_src, above_dst, (group, up), has_up, has_down
            )

        def send_rows(edge, dst):
            return remote(edge.at[0], dst.at[0], (group - 1, slab), has_prev, has_next) + remote(
                edge.at[1], dst.at[1], (group + 1, slab), has_next, has_prev
            )

        rims = ((0, 16, has_next), (1, 6, has_prev))
        own = pl.ds(8, tile)
        cut_edges = lambda edge, at, pad_ref, plane: (
            edge.__setitem__((0, at), pad_ref[plane, 8:10, :]),
            edge.__setitem__((1, at), pad_ref[plane, tile + 6 : tile + 8, :]),
        )

        des_planes = send_z(
            design_in.at[pl.ds(0, 2)], des_z.at[1], design_in.at[pl.ds(planes - 2, 2)], des_z.at[0]
        )

        face_of = lambda faces, plane: faces.at[plane // 3, plane % 3, pl.ds(0, rows), :]

        def face_copy(way, plane, where, stop=None, source=None, sent=None):
            if source is None:
                source = (
                    disp.at[plane // 3, plane % 3, 0]
                    if way == 0
                    else disp.at[half + plane // 3, plane % 3, planes - 1]
                )
            return pltpu.make_async_remote_copy(
                src_ref=source,
                dst_ref=face_of((high_face, low_face)[way], plane) if stop is None else relay.at[stop],
                send_sem=face_send.at[way, plane] if sent is None else sent,
                recv_sem=face_recv.at[way, plane] if stop is None else relay_recv.at[stop],
                device_id=(group, where),
                device_id_type=MESH,
            )

        ways = (
            (0, down, has_down, has_up, RELAY_DOWN, 0, run_down, run - 1),
            (1, up, has_up, has_down, RELAY_UP, RUN - 1, run_up, run + RUN),
        )
        for plane in (1, 2, 5, 4, 0, 3):
            for way, where, send_if, _, relays, end, crosses, _ in ways:
                if plane in relays:
                    at, stop = relays[plane]
                    pl.when(crosses & (place == end))(face_copy(way, plane, run + at, stop).start)
                    pl.when(place != end)(face_copy(way, plane, where).start)
                else:
                    pl.when(send_if)(face_copy(way, plane, where).start)

        def pass_on(stop):
            for way, _, _, _, relays, _, crosses, target in ways:
                for plane, (at, slot) in relays.items():
                    if slot == stop:

                        def forward():
                            copy = face_copy(way, plane, target, source=relay.at[stop], sent=relay_send.at[stop])
                            face_copy(way, plane, target, stop).wait_recv()
                            copy.start()

                        pl.when(crosses & (place == at))(forward)

        for copy in small:
            copy.wait()

        zero_rows = jnp.zeros((8, cols), jnp.float32)
        for comp in range(3):
            for slot in range(slots):
                for plane in range(planes):
                    field[slot, comp, plane, rows : rows + 8, :] = zero_rows
            for slot in range(half):
                low_face[slot, comp, rows : rows + 8, :] = zero_rows
                high_face[slot, comp, rows : rows + 8, :] = zero_rows

        def clear(face_ref):
            for slot in range(half):
                for comp in range(3):
                    face_ref[slot, comp, 0:rows, :] = jnp.zeros((rows, cols), jnp.float32)

        pl.when(slab == 0)(lambda: clear(low_face))
        pl.when(slab == slabs - 1)(lambda: clear(high_face))

        coef = []
        for slot in range(slots):
            node = slot_node[slot]
            index = jnp.clip(node, 0, node_weight.shape[0] - 1)
            value = node_weight[index] * node_stiffness[index]
            coef.append(jnp.where(node < node_weight.shape[0], value, 0.0))

        last = lax.broadcasted_iota(jnp.int32, (8, cols), 1) == cols - 1
        next_rows = lax.broadcasted_iota(jnp.int32, (8, cols), 0) == 0

        def modes_of(plane_ref, block):
            def load(comp):
                return [plane_ref[comp, pl.ds(pl.multiple_of((block + k) * 8, 8), 8), :] for k in range(2)]

            return plane_modes(load, next_rows, last)

        for slot in range(slots):
            loads[slot].wait()

            def block_step(block, carry):
                here = modes_of(field.at[slot, :, 0], block)
                for layer in range(planes - 1):
                    above = modes_of(field.at[slot, :, layer + 1], block)
                    value = coef[slot] * layer_energy(here, above)
                    spot = (lax.rem(block, 2), lax.div(block, 2), layer)
                    in_sums[spot] = value if slot == 0 else in_sums[spot] + value
                    here = above
                return carry

            lax.fori_loop(0, rows // 8, block_step, 0)
            if slot < 2:
                pass_on(slot)
            if slot == 1:
                arrive(des_planes)
                des_pad[pl.ds(2, planes), own, :] = design[...]
                des_pad[pl.ds(0, 2), own, :] = jnp.where(has_down, des_z[0], 0.0)
                des_pad[pl.ds(planes + 2, 2), own, :] = jnp.where(has_up, des_z[1], 0.0)
                for plane in range(planes + 4):
                    cut_edges(des_edge, plane, des_pad, plane)
                des_rows = send_rows(des_edge, des_y)

        def swap(sums, mate_sums):
            return remote(sums.at[1 - core], mate_sums, mate)

        def spread(sums, mate_sums, pair, peer_sums):
            for index in range(chips):
                pair[index] = sums[core, index] + mate_sums[index]
            copies = []
            for k in range(1, chips):
                copies += remote(pair.at[lax.rem(chip + k, chips)], peer_sums.at[k - 1], peers[k - 1])
            return copies

        def total(pair, peer_sums, layer):
            return pair[chip, layer] + add_up([peer_sums[k, layer] for k in range(chips - 1)])

        in_swap = swap(in_sums, in_mate)

        arrive(des_rows)
        for rim, first, cond in rims:
            des_pad[:, pl.ds(first, 2), :] = jnp.where(cond, des_y[rim], 0.0)
        row_at = lax.broadcasted_iota(jnp.int32, (tile, cols), 0) + group * tile
        ones = []
        for dy in range(3):
            within = lambda y: jnp.where((y >= 0) & (y < groups * tile), 1.0, 0.0)
            ones.append(within(row_at) if dy == 0 else within(row_at - dy) + within(row_at + dy))
        base = math.tanh(BETA * ETA)
        scale = base + math.tanh(BETA * (1.0 - ETA))
        filt_rows = [row_sums(des_pad, p) for p in range(planes + 4)]
        for plane in range(planes):
            z = slab * planes + plane
            here = lambda d: jnp.where((z + d >= 0) & (z + d < slabs * planes), 1.0, 0.0)
            gains = [1.0, here(-1) + here(1), here(-2) + here(2)]
            cover = smooth([[v * gain for v in ones] for gain in gains], cols)
            filtered = smooth(z_sums(filt_rows, plane + 2), cols) / cover
            level = jnp.tanh(BETA * (filtered - ETA))
            projected = (base + level) / scale
            slope = BETA * (1.0 - level * level) / scale
            fac[plane] = (-3.0 * (1.0 - E_FLOOR)) * (projected * projected) * slope / cover
        factor = remote(fac.at[planes - 1], fac_low, (group, up), has_up, has_down)
        arrive(in_swap)
        in_spread = spread(in_sums, in_mate, in_pair, in_peers)

        def face_energy(slot):
            for comp in range(3):
                for way, where, _, recv_if, *_ in ways:
                    pl.when(recv_if)(face_copy(way, 3 * slot + comp, where).wait_recv)

            def face_step(block, carry):
                spot = lambda layer: (lax.rem(block, 2), lax.div(block, 2), layer)
                lower = layer_energy(
                    modes_of(low_face.at[slot], block), modes_of(field.at[half + slot, :, 0], block)
                )
                value = coef[half + slot] * lower
                face_sums[spot(0)] = value if slot == 0 else face_sums[spot(0)] + value
                upper = layer_energy(
                    modes_of(field.at[slot, :, planes - 1], block), modes_of(high_face.at[slot], block)
                )
                value = coef[slot] * upper
                face_sums[spot(1)] = value if slot == 0 else face_sums[spot(1)] + value
                return carry

            lax.fori_loop(0, rows // 8, face_step, 0)

        def top_energy():
            def top_step(block, carry):
                spot = (lax.rem(block, 2), lax.div(block, 2), 1)
                zero = jnp.zeros((8, cols), jnp.float32)
                for slot in range(half, slots):
                    modes = modes_of(field.at[slot, :, planes - 1], block)
                    face_sums[spot] += coef[slot] * layer_energy(modes, [(zero,) * 4] * 3)
                return carry

            lax.fori_loop(0, rows // 8, top_step, 0)

        face_energy(0)
        pl.when(slab == slabs - 1)(top_energy)

        for slot in range(1, half):
            face_energy(slot)
        face_swap = swap(face_sums, face_mate)

        def corners(edge, lower, upper, dst):
            copies = []
            for rim, step, send_if, recv_if in ((0, -1, has_prev, has_next), (1, 1, has_next, has_prev)):
                for part, side, where, send_s, recv_s in (
                    (lower, 1, down, has_down, has_up),
                    (upper, 0, up, has_up, has_down),
                ):
                    copies += remote(
                        edge.at[rim, part], dst[side].at[rim], (group + step, where), send_if & send_s, recv_if & recv_s
                    )
            return copies

        arrive(in_spread)
        inner = planes - 1
        for layer in range(inner):
            sen[layer] = total(in_pair, in_peers, layer) * fac[layer]
        sen_edge[0, 0:inner] = sen[:, 0:2, :]
        sen_edge[1, 0:inner] = sen[:, tile - 2 : tile, :]
        halo = send_z(sen.at[pl.ds(0, 2)], sen_high, sen.at[inner - 1], sen_low)
        halo += corners(sen_edge, pl.ds(0, 2), inner - 1, (sen_cl, sen_ch))

        arrive(face_swap)
        face_spread = spread(face_sums, face_mate, face_pair, face_peers)
        sen_pad[pl.ds(2, inner), own, :] = sen[...]
        arrive(factor)
        arrive(face_spread)
        late[0] = total(face_pair, face_peers, 0) * jnp.where(has_down, fac_low[...], 0.0)
        late[1] = total(face_pair, face_peers, 1) * fac[inner]
        late_halo = send_z(late.at[0], late_z.at[1], late.at[1], late_z.at[0])
        sen_edge[0, inner : inner + 2] = late[:, 0:2, :]
        sen_edge[1, inner : inner + 2] = late[:, tile - 2 : tile, :]
        late_halo += corners(sen_edge, inner, inner + 1, (late_c.at[0], late_c.at[1]))
        late_halo += send_rows(sen_edge, sen_y)

        arrive(halo)
        sen_pad[0, own, :] = jnp.where(has_down, sen_low[...], 0.0)
        sen_pad[pl.ds(planes + 2, 2), own, :] = jnp.where(has_up, sen_high[...], 0.0)
        for rim, first, cond in rims:
            span = pl.ds(first, 2)
            sen_pad[0, span, :] = jnp.where(cond & has_down, sen_cl[rim], 0.0)
            sen_pad[pl.ds(planes + 2, 2), span, :] = jnp.where(cond & has_up, sen_ch[rim], 0.0)
        arrive(late_halo)
        sen_pad[1, own, :] = jnp.where(has_down, late[0] + late_z[0], 0.0)
        sen_pad[planes + 1, own, :] = late[1] + jnp.where(has_up, late_z[1], 0.0)
        for rim, first, cond in rims:
            span = pl.ds(first, 2)
            sen_pad[1, span, :] = jnp.where(cond & has_down, sen_y[rim, inner] + late_c[0, rim], 0.0)
            sen_pad[pl.ds(2, inner), span, :] = jnp.where(cond, sen_y[rim, 0:inner], 0.0)
            sen_pad[planes + 1, span, :] = jnp.where(cond, sen_y[rim, inner + 1], 0.0) + jnp.where(
                cond & has_up, late_c[1, rim], 0.0
            )
        sens_rows = [row_sums(sen_pad, p) for p in range(planes + 4)]
        for plane in range(planes):
            out[plane] = smooth(z_sums(sens_rows, plane + 2), cols)

        for copy, send_if, _ in started:
            when(send_if, copy.wait_send)
        for plane in range(3 * half):
            for way, where, send_if, *_ in ways:
                pl.when(send_if)(face_copy(way, plane, where).wait_send)
        for way, where, _, _, relays, _, crosses, _ in ways:
            for plane, (at, stop) in relays.items():
                copy = face_copy(way, plane, where, source=relay.at[stop], sent=relay_send.at[stop])
                pl.when(crosses & (place == at))(copy.wait_send)

    vmem = lambda *shape: pltpu.VMEM(shape, jnp.float32)
    copies = 2 + 2 + 1 + 2 * chips + 6 + 8
    inner = planes - 1
    scratch = [
        pltpu.SMEM((slots,), jnp.int32),
        pltpu.SMEM((nodes,), jnp.float32),
        pltpu.SMEM((nodes,), jnp.float32),
        vmem(planes, tile, cols),
        vmem(slots, 3, planes, rows + 8, cols),
        vmem(half, 3, rows + 8, cols),
        vmem(half, 3, rows + 8, cols),
        vmem(2, rows, cols),
        vmem(planes + 4, 24, cols),
        vmem(2, 2, tile, cols),
        vmem(2, planes + 4, 2, cols),
        vmem(2, planes + 4, 2, cols),
        vmem(planes, tile, cols),
        vmem(tile, cols),
        vmem(2, chips, inner, tile, cols),
        vmem(chips, inner, tile, cols),
        vmem(chips, inner, tile, cols),
        vmem(chips - 1, inner, tile, cols),
        vmem(inner, tile, cols),
        vmem(planes + 4, 24, cols),
        vmem(tile, cols),
        vmem(2, tile, cols),
        vmem(2, 2, cols),
        vmem(2, 2, 2, cols),
        vmem(2, planes + 1, 2, cols),
        vmem(2, planes + 1, 2, cols),
        vmem(2, chips, 2, tile, cols),
        vmem(chips, 2, tile, cols),
        vmem(chips, 2, tile, cols),
        vmem(chips - 1, 2, tile, cols),
        vmem(2, tile, cols),
        vmem(2, tile, cols),
        vmem(2, 2, 2, cols),
        pltpu.SemaphoreType.DMA((slots,)),
        pltpu.SemaphoreType.DMA((4,)),
        pltpu.SemaphoreType.DMA((copies,)),
        pltpu.SemaphoreType.DMA((copies,)),
        pltpu.SemaphoreType.DMA((2, 3 * half)),
        pltpu.SemaphoreType.DMA((2, 3 * half)),
        pltpu.SemaphoreType.DMA((2,)),
        pltpu.SemaphoreType.DMA((2,)),
    ]
    return kernel, scratch


def solution(mesh):
    groups, slabs = mesh.shape["nodes"], mesh.shape["space"]

    def per_device(displacement, slot_node, node_weight, node_stiffness, design):
        slots, _, planes, rows, cols = displacement.shape
        kernel, scratch = make_kernel(groups, slabs, node_weight.shape[0], slots, planes, rows, cols, design.shape[1])
        return pl.pallas_call(
            kernel,
            out_shape=jax.ShapeDtypeStruct(design.shape, jnp.float32),
            in_specs=[pl.BlockSpec(memory_space=pltpu.HBM)] * 5,
            out_specs=pl.BlockSpec(memory_space=pltpu.VMEM),
            scratch_shapes=scratch,
            compiler_params=pltpu.CompilerParams(
                collective_id=0, has_side_effects=True, vmem_limit_bytes=60 * 2**20
            ),
            cost_estimate=pl.CostEstimate(flops=40_000_000, bytes_accessed=4_000_000, transcendentals=8192),
            name="sensitivity",
        )(displacement, slot_node, node_weight, node_stiffness, design)

    return jax.shard_map(
        per_device,
        mesh=mesh,
        in_specs=(
            P("nodes", None, "space", None, None),
            P("nodes"),
            P(),
            P(),
            P("space", "nodes", None),
        ),
        out_specs=P("space", "nodes", None),
        check_vma=False,
    )
```

```python
import math

import jax
import jax.numpy as jnp
from jax import lax
from jax.experimental import pallas as pl
from jax.experimental.pallas import tpu as pltpu
from jax.sharding import PartitionSpec as P

POISSON = 0.3
E_FLOOR = 0.001
BETA = 8.0
ETA = 0.5
RADIUS = 2.5
MESH = pl.DeviceIdType.MESH
RUN = 4
RELAY_DOWN = {1: (3, 0), 4: (3, 1), 2: (1, 0), 5: (2, 0)}
RELAY_UP = {1: (0, 0), 4: (0, 1), 2: (2, 1), 5: (1, 1)}


def weight(dz, dy, dx):
    return max(0.0, RADIUS - math.sqrt(dz * dz + dy * dy + dx * dx))


def add_up(terms):
    total = None
    for term in terms:
        total = term if total is None else total + term
    return total


def next_lane(v, last):
    return jnp.where(last, 0.0, pltpu.roll(v, v.shape[1] - 1, 1))


def plane_modes(load, next_rows, last):
    modes = []
    for comp in range(3):
        here, below = load(comp)
        up = pltpu.roll(jnp.where(next_rows, below, here), 7, 0)
        ysum, ydif = up + here, up - here
        ysum_x, ydif_x = next_lane(ysum, last), next_lane(ydif, last)
        modes.append((ysum_x + ysum, ysum_x - ysum, ydif_x + ydif, ydif_x - ydif))
    return modes


def layer_energy(low, high):
    lam = POISSON / ((1.0 + POISSON) * (1.0 - 2.0 * POISSON))
    shear = 1.0 / (2.0 * (1.0 + POISSON))
    sums = [[lo + hi for lo, hi in zip(a, b)] for a, b in zip(low, high)]
    difs = [[hi - lo for lo, hi in zip(a, b)] for a, b in zip(low, high)]
    (_, ax, ay, axy), (_, bx, by, bxy), (_, cx, cy, cxy) = sums
    (az, azx, ayz, axyz), (bz, bzx, byz, bxyz), (cz, czx, cyz, cxyz) = difs
    sq = lambda v: v * v
    div = sq(ax + by + cz)
    diag = sq(ax) + sq(by) + sq(cz)
    skew = sq(ay + bx) + sq(az + cx) + sq(bz + cy)
    even = sq(bxy + czx) + sq(axy + cyz) + sq(azx + byz)
    odd = sq(bxy - czx) + sq(axy - cyz) + sq(azx - byz)
    mixed = sq(ayz + bzx) + sq(ayz + cxy) + sq(bzx + cxy)
    high_order = sq(axyz) + sq(bxyz) + sq(cxyz)
    return (
        (lam / 16.0) * div
        + (2.0 * shear / 16.0) * diag
        + (shear / 16.0) * skew
        + ((lam + 1.5 * shear) / 48.0) * even
        + (1.5 * shear / 48.0) * odd
        + (shear / 48.0) * mixed
        + ((lam + 4.0 * shear) / 144.0) * high_order
    )


def smooth(windows, cols):
    lanes = lax.broadcasted_iota(jnp.int32, windows[0][0].shape, 1)
    total = None
    for dx in range(3):
        part = add_up(
            [weight(i, j, dx) * windows[i][j] for i in range(3) for j in range(3) if weight(i, j, dx) > 0.0]
        )
        if dx > 0:
            right = jnp.where(lanes < cols - dx, pltpu.roll(part, cols - dx, 1), 0.0)
            left = jnp.where(lanes >= dx, pltpu.roll(part, dx, 1), 0.0)
            part = left + right
        total = part if total is None else total + part
    return total


def row_sums(field, plane):
    at = lambda first: field[plane, first : first + 8, :]
    return [at(8), at(7) + at(9), at(6) + at(10)]


def z_sums(rows, plane):
    return [
        rows[plane],
        [a + b for a, b in zip(rows[plane - 1], rows[plane + 1])],
        [a + b for a, b in zip(rows[plane - 2], rows[plane + 2])],
    ]


def make_kernel(groups, slabs, nodes, slots, planes, rows, cols, tile):
    half = slots // 2
    chips = groups // 2

    def kernel(
        disp, slot_node_in, node_weight_in, node_stiffness_in, design_in, out,
        slot_node, node_weight, node_stiffness, design, field, kept, low_face, high_face, relay,
        des_pad, des_z, des_edge, des_y, fac, fac_low,
        in_sums, in_mate, in_pair, in_peers, sen, sen_pad, sen_low, sen_high, sen_cl, sen_ch, sen_edge, sen_y,
        face_sums, face_mate, face_pair, face_peers, late, late_z, late_c,
        load_sem, small_sem, send_sem, recv_sem, face_send, face_recv, relay_send, relay_recv,
    ):
        group = lax.axis_index("nodes")
        slab = lax.axis_index("space")
        core = lax.rem(group, 2)
        chip = lax.div(group, 2)
        place = lax.rem(slab, RUN)
        run = slab - place
        down, up = slab - 1, slab + 1
        has_prev, has_next = group > 0, group < groups - 1
        has_down, has_up = slab > 0, slab < slabs - 1
        run_down, run_up = run > 0, run < slabs - RUN
        mate = (group + 1 - 2 * core, slab)
        peers = [(2 * lax.rem(chip + k, chips) + core, slab) for k in range(1, chips)]

        def when(condition, action):
            if condition is None:
                action()
            else:
                pl.when(condition)(action)

        aside = group + 2 * core - 1
        partners = [((group, down), run_down & (place == 0)), ((group, up), run_up & (place == RUN - 1))]
        partners += [((group, run + lax.rem(place + k, RUN)), None) for k in range(1, RUN)]
        partners += [(mate, None)] + [(peer, None) for peer in peers]
        partners.append(((aside, slab), (aside >= 0) & (aside < groups)))
        barrier = pltpu.get_barrier_semaphore()
        for device, cond in partners:
            when(cond, lambda: pl.semaphore_signal(barrier, inc=1, device_id=device, device_id_type=MESH))
        loads = []
        for slot in range(slots):
            load = pltpu.make_async_copy(
                disp.at[slot], field.at[slot, :, :, pl.ds(0, rows), :], load_sem.at[slot]
            )
            load.start()
            loads.append(load)
        small = []
        for number, (source, target) in enumerate(
            (
                (design_in, design),
                (slot_node_in, slot_node),
                (node_weight_in, node_weight),
                (node_stiffness_in, node_stiffness),
            )
        ):
            small.append(pltpu.make_async_copy(source, target, small_sem.at[number]))
            small[-1].start()
        pl.semaphore_wait(barrier, sum(1 if cond is None else cond.astype(jnp.int32) for _, cond in partners))

        started = []

        def remote(src, dst, device, send_if=None, recv_if=None):
            number = len(started)
            copy = pltpu.make_async_remote_copy(
                src_ref=src, dst_ref=dst, send_sem=send_sem.at[number], recv_sem=recv_sem.at[number],
                device_id=device, device_id_type=MESH,
            )
            started.append((copy, send_if, recv_if))
            when(send_if, copy.start)
            return started[-1:]

        def arrive(copies):
            for copy, _, recv_if in copies:
                when(recv_if, copy.wait_recv)

        def send_z(below_src, below_dst, above_src, above_dst):
            return remote(below_src, below_dst, (group, down), has_down, has_up) + remote(
                above_src, above_dst, (group, up), has_up, has_down
            )

        def send_rows(edge, dst):
            return remote(edge.at[0], dst.at[0], (group - 1, slab), has_prev, has_next) + remote(
                edge.at[1], dst.at[1], (group + 1, slab), has_next, has_prev
            )

        rims = ((0, 16, has_next), (1, 6, has_prev))
        own = pl.ds(8, tile)
        cut_edges = lambda edge, at, pad_ref, plane: (
            edge.__setitem__((0, at), pad_ref[plane, 8:10, :]),
            edge.__setitem__((1, at), pad_ref[plane, tile + 6 : tile + 8, :]),
        )

        des_planes = send_z(
            design_in.at[pl.ds(0, 2)], des_z.at[1], design_in.at[pl.ds(planes - 2, 2)], des_z.at[0]
        )

        face_of = lambda faces, plane: faces.at[plane // 3, plane % 3, pl.ds(0, rows), :]

        def face_copy(way, plane, where, stop=None, source=None, sent=None):
            if source is None:
                source = (
                    disp.at[plane // 3, plane % 3, 0]
                    if way == 0
                    else disp.at[half + plane // 3, plane % 3, planes - 1]
                )
            return pltpu.make_async_remote_copy(
                src_ref=source,
                dst_ref=face_of((high_face, low_face)[way], plane) if stop is None else relay.at[stop],
                send_sem=face_send.at[way, plane] if sent is None else sent,
                recv_sem=face_recv.at[way, plane] if stop is None else relay_recv.at[stop],
                device_id=(group, where),
                device_id_type=MESH,
            )

        ways = (
            (0, down, has_down, has_up, RELAY_DOWN, 0, run_down, run - 1),
            (1, up, has_up, has_down, RELAY_UP, RUN - 1, run_up, run + RUN),
        )
        for plane in (0, 1, 2, 5, 4, 3):
            for way, where, _, _, relays, end, crosses, _ in ways:
                copy = (
                    face_copy(way, plane, run + relays[plane][0], relays[plane][1])
                    if plane in relays
                    else face_copy(way, plane, where)
                )
                pl.when(crosses & (place == end))(copy.start)
        for plane in range(3 * half):
            for way, where, _, _, _, end, _, _ in ways:
                pl.when(place != end)(face_copy(way, plane, where).start)

        def pass_on(stop):
            for way, _, _, _, relays, _, crosses, target in ways:
                for plane, (at, slot) in relays.items():
                    if slot == stop:

                        def forward():
                            copy = face_copy(way, plane, target, source=relay.at[stop], sent=relay_send.at[stop])
                            face_copy(way, plane, target, stop).wait_recv()
                            copy.start()

                        pl.when(crosses & (place == at))(forward)

        for copy in small:
            copy.wait()

        zero_rows = jnp.zeros((8, cols), jnp.float32)
        for comp in range(3):
            for slot in range(slots):
                for plane in range(planes):
                    field[slot, comp, plane, rows : rows + 8, :] = zero_rows
            for slot in range(half):
                low_face[slot, comp, rows : rows + 8, :] = zero_rows
                high_face[slot, comp, rows : rows + 8, :] = zero_rows

        def clear(face_ref):
            for slot in range(half):
                for comp in range(3):
                    face_ref[slot, comp, 0:rows, :] = jnp.zeros((rows, cols), jnp.float32)

        pl.when(slab == 0)(lambda: clear(low_face))
        pl.when(slab == slabs - 1)(lambda: clear(high_face))

        coef = []
        for slot in range(slots):
            node = slot_node[slot]
            index = jnp.clip(node, 0, node_weight.shape[0] - 1)
            value = node_weight[index] * node_stiffness[index]
            coef.append(jnp.where(node < node_weight.shape[0], value, 0.0))

        last = lax.broadcasted_iota(jnp.int32, (8, cols), 1) == cols - 1
        next_rows = lax.broadcasted_iota(jnp.int32, (8, cols), 0) == 0

        def modes_of(plane_ref, block):
            def load(comp):
                return [plane_ref[comp, pl.ds(pl.multiple_of((block + k) * 8, 8), 8), :] for k in range(2)]

            return plane_modes(load, next_rows, last)

        def keep(slot, block, modes):
            for comp in range(3):
                for mode in range(4):
                    kept[slot, comp, mode, pl.ds(pl.multiple_of(block * 8, 8), 8), :] = modes[comp][mode]

        def kept_modes(slot, block):
            span = pl.ds(pl.multiple_of(block * 8, 8), 8)
            return [[kept[slot, comp, mode, span, :] for mode in range(4)] for comp in range(3)]

        for slot in range(slots):
            loads[slot].wait()

            def block_step(block, carry):
                here = modes_of(field.at[slot, :, 0], block)
                if slot >= half:
                    keep(slot, block, here)
                for layer in range(planes - 1):
                    above = modes_of(field.at[slot, :, layer + 1], block)
                    value = coef[slot] * layer_energy(here, above)
                    spot = (lax.rem(block, 2), lax.div(block, 2), layer)
                    in_sums[spot] = value if slot == 0 else in_sums[spot] + value
                    here = above
                if slot < half:
                    keep(slot, block, here)
                return carry

            lax.fori_loop(0, rows // 8, block_step, 0, unroll=2)
            if slot < 2:
                pass_on(slot)
            if slot == 1:
                arrive(des_planes)
                des_pad[pl.ds(2, planes), own, :] = design[...]
                des_pad[pl.ds(0, 2), own, :] = jnp.where(has_down, des_z[0], 0.0)
                des_pad[pl.ds(planes + 2, 2), own, :] = jnp.where(has_up, des_z[1], 0.0)
                for plane in range(planes + 4):
                    cut_edges(des_edge, plane, des_pad, plane)
                des_rows = send_rows(des_edge, des_y)

        def swap(sums, mate_sums):
            return remote(sums.at[1 - core], mate_sums, mate)

        def spread(sums, mate_sums, pair, peer_sums):
            for index in range(chips):
                pair[index] = sums[core, index] + mate_sums[index]
            copies = []
            for k in range(1, chips):
                copies += remote(pair.at[lax.rem(chip + k, chips)], peer_sums.at[k - 1], peers[k - 1])
            return copies

        def total(pair, peer_sums, layer):
            return pair[chip, layer] + add_up([peer_sums[k, layer] for k in range(chips - 1)])

        in_swap = swap(in_sums, in_mate)

        arrive(des_rows)
        for rim, first, cond in rims:
            des_pad[:, pl.ds(first, 2), :] = jnp.where(cond, des_y[rim], 0.0)
        row_at = lax.broadcasted_iota(jnp.int32, (tile, cols), 0) + group * tile
        ones = []
        for dy in range(3):
            within = lambda y: jnp.where((y >= 0) & (y < groups * tile), 1.0, 0.0)
            ones.append(within(row_at) if dy == 0 else within(row_at - dy) + within(row_at + dy))
        base = math.tanh(BETA * ETA)
        scale = base + math.tanh(BETA * (1.0 - ETA))
        filt_rows = [row_sums(des_pad, p) for p in range(planes + 4)]
        for plane in range(planes):
            z = slab * planes + plane
            here = lambda d: jnp.where((z + d >= 0) & (z + d < slabs * planes), 1.0, 0.0)
            gains = [1.0, here(-1) + here(1), here(-2) + here(2)]
            cover = smooth([[v * gain for v in ones] for gain in gains], cols)
            filtered = smooth(z_sums(filt_rows, plane + 2), cols) / cover
            level = jnp.tanh(BETA * (filtered - ETA))
            projected = (base + level) / scale
            slope = BETA * (1.0 - level * level) / scale
            fac[plane] = (-3.0 * (1.0 - E_FLOOR)) * (projected * projected) * slope / cover
        factor = remote(fac.at[planes - 1], fac_low, (group, up), has_up, has_down)
        arrive(in_swap)
        in_spread = spread(in_sums, in_mate, in_pair, in_peers)

        def face_energy(slot):
            for comp in range(3):
                for way, where, _, recv_if, *_ in ways:
                    pl.when(recv_if)(face_copy(way, 3 * slot + comp, where).wait_recv)

            def face_step(block, carry):
                spot = lambda layer: (lax.rem(block, 2), lax.div(block, 2), layer)
                lower = layer_energy(modes_of(low_face.at[slot], block), kept_modes(half + slot, block))
                value = coef[half + slot] * lower
                face_sums[spot(0)] = value if slot == 0 else face_sums[spot(0)] + value
                upper = layer_energy(kept_modes(slot, block), modes_of(high_face.at[slot], block))
                value = coef[slot] * upper
                face_sums[spot(1)] = value if slot == 0 else face_sums[spot(1)] + value
                return carry

            lax.fori_loop(0, rows // 8, face_step, 0, unroll=4)

        def top_energy():
            def top_step(block, carry):
                spot = (lax.rem(block, 2), lax.div(block, 2), 1)
                zero = jnp.zeros((8, cols), jnp.float32)
                for slot in range(half, slots):
                    modes = modes_of(field.at[slot, :, planes - 1], block)
                    face_sums[spot] += coef[slot] * layer_energy(modes, [(zero,) * 4] * 3)
                return carry

            lax.fori_loop(0, rows // 8, top_step, 0)

        face_energy(0)
        pl.when(slab == slabs - 1)(top_energy)

        for slot in range(1, half):
            face_energy(slot)
        face_swap = swap(face_sums, face_mate)

        def corners(edge, lower, upper, dst):
            copies = []
            for rim, step, send_if, recv_if in ((0, -1, has_prev, has_next), (1, 1, has_next, has_prev)):
                for part, side, where, send_s, recv_s in (
                    (lower, 1, down, has_down, has_up),
                    (upper, 0, up, has_up, has_down),
                ):
                    copies += remote(
                        edge.at[rim, part], dst[side].at[rim], (group + step, where), send_if & send_s, recv_if & recv_s
                    )
            return copies

        arrive(in_spread)
        inner = planes - 1
        for layer in range(inner):
            sen[layer] = total(in_pair, in_peers, layer) * fac[layer]
        sen_edge[0, 0:inner] = sen[:, 0:2, :]
        sen_edge[1, 0:inner] = sen[:, tile - 2 : tile, :]
        halo = send_z(sen.at[pl.ds(0, 2)], sen_high, sen.at[inner - 1], sen_low)
        halo += corners(sen_edge, pl.ds(0, 2), inner - 1, (sen_cl, sen_ch))

        arrive(face_swap)
        face_spread = spread(face_sums, face_mate, face_pair, face_peers)
        sen_pad[pl.ds(2, inner), own, :] = sen[...]
        arrive(factor)
        arrive(face_spread)
        late[0] = total(face_pair, face_peers, 0) * jnp.where(has_down, fac_low[...], 0.0)
        late[1] = total(face_pair, face_peers, 1) * fac[inner]
        late_halo = send_z(late.at[0], late_z.at[1], late.at[1], late_z.at[0])
        sen_edge[0, inner : inner + 2] = late[:, 0:2, :]
        sen_edge[1, inner : inner + 2] = late[:, tile - 2 : tile, :]
        late_halo += corners(sen_edge, inner, inner + 1, (late_c.at[0], late_c.at[1]))
        late_halo += send_rows(sen_edge, sen_y)

        arrive(halo)
        sen_pad[0, own, :] = jnp.where(has_down, sen_low[...], 0.0)
        sen_pad[pl.ds(planes + 2, 2), own, :] = jnp.where(has_up, sen_high[...], 0.0)
        for rim, first, cond in rims:
            span = pl.ds(first, 2)
            sen_pad[0, span, :] = jnp.where(cond & has_down, sen_cl[rim], 0.0)
            sen_pad[pl.ds(planes + 2, 2), span, :] = jnp.where(cond & has_up, sen_ch[rim], 0.0)
        arrive(late_halo)
        sen_pad[1, own, :] = jnp.where(has_down, late[0] + late_z[0], 0.0)
        sen_pad[planes + 1, own, :] = late[1] + jnp.where(has_up, late_z[1], 0.0)
        for rim, first, cond in rims:
            span = pl.ds(first, 2)
            sen_pad[1, span, :] = jnp.where(cond & has_down, sen_y[rim, inner] + late_c[0, rim], 0.0)
            sen_pad[pl.ds(2, inner), span, :] = jnp.where(cond, sen_y[rim, 0:inner], 0.0)
            sen_pad[planes + 1, span, :] = jnp.where(cond, sen_y[rim, inner + 1], 0.0) + jnp.where(
                cond & has_up, late_c[1, rim], 0.0
            )
        sens_rows = [row_sums(sen_pad, p) for p in range(planes + 4)]
        for plane in range(planes):
            out[plane] = smooth(z_sums(sens_rows, plane + 2), cols)

        for copy, send_if, _ in started:
            when(send_if, copy.wait_send)
        for plane in range(3 * half):
            for way, where, send_if, *_ in ways:
                pl.when(send_if)(face_copy(way, plane, where).wait_send)
        for way, where, _, _, relays, _, crosses, _ in ways:
            for plane, (at, stop) in relays.items():
                copy = face_copy(way, plane, where, source=relay.at[stop], sent=relay_send.at[stop])
                pl.when(crosses & (place == at))(copy.wait_send)

    vmem = lambda *shape: pltpu.VMEM(shape, jnp.float32)
    copies = 2 + 2 + 1 + 2 * chips + 6 + 8
    inner = planes - 1
    scratch = [
        pltpu.SMEM((slots,), jnp.int32),
        pltpu.SMEM((nodes,), jnp.float32),
        pltpu.SMEM((nodes,), jnp.float32),
        vmem(planes, tile, cols),
        vmem(slots, 3, planes, rows + 8, cols),
        vmem(slots, 3, 4, rows, cols),
        vmem(half, 3, rows + 8, cols),
        vmem(half, 3, rows + 8, cols),
        vmem(2, rows, cols),
        vmem(planes + 4, 24, cols),
        vmem(2, 2, tile, cols),
        vmem(2, planes + 4, 2, cols),
        vmem(2, planes + 4, 2, cols),
        vmem(planes, tile, cols),
        vmem(tile, cols),
        vmem(2, chips, inner, tile, cols),
        vmem(chips, inner, tile, cols),
        vmem(chips, inner, tile, cols),
        vmem(chips - 1, inner, tile, cols),
        vmem(inner, tile, cols),
        vmem(planes + 4, 24, cols),
        vmem(tile, cols),
        vmem(2, tile, cols),
        vmem(2, 2, cols),
        vmem(2, 2, 2, cols),
        vmem(2, planes + 1, 2, cols),
        vmem(2, planes + 1, 2, cols),
        vmem(2, chips, 2, tile, cols),
        vmem(chips, 2, tile, cols),
        vmem(chips, 2, tile, cols),
        vmem(chips - 1, 2, tile, cols),
        vmem(2, tile, cols),
        vmem(2, tile, cols),
        vmem(2, 2, 2, cols),
        pltpu.SemaphoreType.DMA((slots,)),
        pltpu.SemaphoreType.DMA((4,)),
        pltpu.SemaphoreType.DMA((copies,)),
        pltpu.SemaphoreType.DMA((copies,)),
        pltpu.SemaphoreType.DMA((2, 3 * half)),
        pltpu.SemaphoreType.DMA((2, 3 * half)),
        pltpu.SemaphoreType.DMA((2,)),
        pltpu.SemaphoreType.DMA((2,)),
    ]
    return kernel, scratch


def solution(mesh):
    groups, slabs = mesh.shape["nodes"], mesh.shape["space"]

    def per_device(displacement, slot_node, node_weight, node_stiffness, design):
        slots, _, planes, rows, cols = displacement.shape
        kernel, scratch = make_kernel(groups, slabs, node_weight.shape[0], slots, planes, rows, cols, design.shape[1])
        return pl.pallas_call(
            kernel,
            out_shape=jax.ShapeDtypeStruct(design.shape, jnp.float32),
            in_specs=[pl.BlockSpec(memory_space=pltpu.HBM)] * 5,
            out_specs=pl.BlockSpec(memory_space=pltpu.VMEM),
            scratch_shapes=scratch,
            compiler_params=pltpu.CompilerParams(
                collective_id=0, has_side_effects=True, vmem_limit_bytes=60 * 2**20
            ),
            cost_estimate=pl.CostEstimate(flops=40_000_000, bytes_accessed=4_000_000, transcendentals=8192),
            name="sensitivity",
        )(displacement, slot_node, node_weight, node_stiffness, design)

    return jax.shard_map(
        per_device,
        mesh=mesh,
        in_specs=(
            P("nodes", None, "space", None, None),
            P("nodes"),
            P(),
            P(),
            P("space", "nodes", None),
        ),
        out_specs=P("space", "nodes", None),
        check_vma=False,
    )
```

```python
import math

import jax
import jax.numpy as jnp
from jax import lax
from jax.experimental import pallas as pl
from jax.experimental.pallas import tpu as pltpu
from jax.sharding import PartitionSpec as P

POISSON = 0.3
E_FLOOR = 0.001
BETA = 8.0
ETA = 0.5
RADIUS = 2.5
MESH = pl.DeviceIdType.MESH
RUN = 4
RELAY_DOWN = {(1, 0): 3, (1, 1): 3, (4, 0): 1, (4, 1): 2, (2, 0): 1, (2, 1): 1, (5, 0): 2, (5, 1): 2}
RELAY_UP = {(1, 0): 0, (1, 1): 0, (4, 0): 0, (4, 1): 1, (2, 0): 2, (2, 1): 2, (5, 0): 1, (5, 1): 1}
FIRST = ({1, 2, 5}, {1})


def relay_slots():
    used, slots = {}, {}
    for way, relays in enumerate((RELAY_DOWN, RELAY_UP)):
        for (plane, part), at in relays.items():
            slots[way, plane, part] = (at, used.get(at, 0))
            used[at] = used.get(at, 0) + 1
    return slots, max(used.values())


def weight(dz, dy, dx):
    return max(0.0, RADIUS - math.sqrt(dz * dz + dy * dy + dx * dx))


def add_up(terms):
    total = None
    for term in terms:
        total = term if total is None else total + term
    return total


def next_lane(v, last):
    return jnp.where(last, 0.0, pltpu.roll(v, v.shape[1] - 1, 1))


def plane_modes(load, next_rows, last):
    modes = []
    for comp in range(3):
        here, below = load(comp)
        up = pltpu.roll(jnp.where(next_rows, below, here), 7, 0)
        ysum, ydif = up + here, up - here
        ysum_x, ydif_x = next_lane(ysum, last), next_lane(ydif, last)
        modes.append((ysum_x + ysum, ysum_x - ysum, ydif_x + ydif, ydif_x - ydif))
    return modes


def layer_energy(low, high):
    lam = POISSON / ((1.0 + POISSON) * (1.0 - 2.0 * POISSON))
    shear = 1.0 / (2.0 * (1.0 + POISSON))
    sums = [[lo + hi for lo, hi in zip(a, b)] for a, b in zip(low, high)]
    difs = [[hi - lo for lo, hi in zip(a, b)] for a, b in zip(low, high)]
    (_, ax, ay, axy), (_, bx, by, bxy), (_, cx, cy, cxy) = sums
    (az, azx, ayz, axyz), (bz, bzx, byz, bxyz), (cz, czx, cyz, cxyz) = difs
    sq = lambda v: v * v
    div = sq(ax + by + cz)
    diag = sq(ax) + sq(by) + sq(cz)
    skew = sq(ay + bx) + sq(az + cx) + sq(bz + cy)
    even = sq(bxy + czx) + sq(axy + cyz) + sq(azx + byz)
    odd = sq(bxy - czx) + sq(axy - cyz) + sq(azx - byz)
    mixed = sq(ayz + bzx) + sq(ayz + cxy) + sq(bzx + cxy)
    high_order = sq(axyz) + sq(bxyz) + sq(cxyz)
    return (
        (lam / 16.0) * div
        + (2.0 * shear / 16.0) * diag
        + (shear / 16.0) * skew
        + ((lam + 1.5 * shear) / 48.0) * even
        + (1.5 * shear / 48.0) * odd
        + (shear / 48.0) * mixed
        + ((lam + 4.0 * shear) / 144.0) * high_order
    )


def smooth(windows, cols):
    lanes = lax.broadcasted_iota(jnp.int32, windows[0][0].shape, 1)
    total = None
    for dx in range(3):
        part = add_up(
            [weight(i, j, dx) * windows[i][j] for i in range(3) for j in range(3) if weight(i, j, dx) > 0.0]
        )
        if dx > 0:
            right = jnp.where(lanes < cols - dx, pltpu.roll(part, cols - dx, 1), 0.0)
            left = jnp.where(lanes >= dx, pltpu.roll(part, dx, 1), 0.0)
            part = left + right
        total = part if total is None else total + part
    return total


def row_sums(field, plane):
    at = lambda first: field[plane, first : first + 8, :]
    return [at(8), at(7) + at(9), at(6) + at(10)]


def z_sums(rows, plane):
    return [
        rows[plane],
        [a + b for a, b in zip(rows[plane - 1], rows[plane + 1])],
        [a + b for a, b in zip(rows[plane - 2], rows[plane + 2])],
    ]


def make_kernel(groups, slabs, nodes, slots, planes, rows, cols, tile):
    half = slots // 2
    chips = groups // 2
    slots_of, stops = relay_slots()

    def kernel(
        disp, slot_node_in, node_weight_in, node_stiffness_in, design_in, out,
        slot_node, node_weight, node_stiffness, design, field, kept, low_face, high_face, relay,
        des_pad, des_z, des_edge, des_y, fac, fac_low,
        in_sums, in_mate, in_pair, in_peers, sen, sen_pad, sen_low, sen_high, sen_cl, sen_ch, sen_edge, sen_y,
        face_sums, face_mate, face_pair, face_peers, late, late_z, late_c,
        load_sem, small_sem, send_sem, recv_sem, face_send, face_recv, relay_send, relay_recv,
    ):
        group = lax.axis_index("nodes")
        slab = lax.axis_index("space")
        core = lax.rem(group, 2)
        chip = lax.div(group, 2)
        place = lax.rem(slab, RUN)
        run = slab - place
        down, up = slab - 1, slab + 1
        has_prev, has_next = group > 0, group < groups - 1
        has_down, has_up = slab > 0, slab < slabs - 1
        run_down, run_up = run > 0, run < slabs - RUN
        mate = (group + 1 - 2 * core, slab)
        peers = [(2 * lax.rem(chip + k, chips) + core, slab) for k in range(1, chips)]

        def when(condition, action):
            if condition is None:
                action()
            else:
                pl.when(condition)(action)

        aside = group + 2 * core - 1
        partners = [((group, down), run_down & (place == 0)), ((group, up), run_up & (place == RUN - 1))]
        partners += [((group, run + lax.rem(place + k, RUN)), None) for k in range(1, RUN)]
        partners += [(mate, None)] + [(peer, None) for peer in peers]
        partners.append(((aside, slab), (aside >= 0) & (aside < groups)))
        barrier = pltpu.get_barrier_semaphore()
        for device, cond in partners:
            when(cond, lambda: pl.semaphore_signal(barrier, inc=1, device_id=device, device_id_type=MESH))
        loads = []
        for slot in range(slots):
            load = pltpu.make_async_copy(
                disp.at[slot], field.at[slot, :, :, pl.ds(0, rows), :], load_sem.at[slot]
            )
            load.start()
            loads.append(load)
        small = []
        for number, (source, target) in enumerate(
            (
                (design_in, design),
                (slot_node_in, slot_node),
                (node_weight_in, node_weight),
                (node_stiffness_in, node_stiffness),
            )
        ):
            small.append(pltpu.make_async_copy(source, target, small_sem.at[number]))
            small[-1].start()
        pl.semaphore_wait(barrier, sum(1 if cond is None else cond.astype(jnp.int32) for _, cond in partners))

        started = []

        def remote(src, dst, device, send_if=None, recv_if=None):
            number = len(started)
            copy = pltpu.make_async_remote_copy(
                src_ref=src, dst_ref=dst, send_sem=send_sem.at[number], recv_sem=recv_sem.at[number],
                device_id=device, device_id_type=MESH,
            )
            started.append((copy, send_if, recv_if))
            when(send_if, copy.start)
            return started[-1:]

        def arrive(copies):
            for copy, _, recv_if in copies:
                when(recv_if, copy.wait_recv)

        def send_z(below_src, below_dst, above_src, above_dst):
            return remote(below_src, below_dst, (group, down), has_down, has_up) + remote(
                above_src, above_dst, (group, up), has_up, has_down
            )

        def send_rows(edge, dst):
            return remote(edge.at[0], dst.at[0], (group - 1, slab), has_prev, has_next) + remote(
                edge.at[1], dst.at[1], (group + 1, slab), has_next, has_prev
            )

        rims = ((0, 16, has_next), (1, 6, has_prev))
        own = pl.ds(8, tile)
        cut_edges = lambda edge, at, pad_ref, plane: (
            edge.__setitem__((0, at), pad_ref[plane, 8:10, :]),
            edge.__setitem__((1, at), pad_ref[plane, tile + 6 : tile + 8, :]),
        )

        des_planes = send_z(
            design_in.at[pl.ds(0, 2)], des_z.at[1], design_in.at[pl.ds(planes - 2, 2)], des_z.at[0]
        )

        def face_copy(way, plane, where, part=None, stop=None, passed=None):
            cut = pl.ds(0, rows) if part is None else pl.ds(part * (rows // 2), rows // 2)
            if passed is not None:
                source = relay.at[passed]
            elif way == 0:
                source = disp.at[plane // 3, plane % 3, 0, cut]
            else:
                source = disp.at[half + plane // 3, plane % 3, planes - 1, cut]
            faces = (high_face, low_face)[way]
            return pltpu.make_async_remote_copy(
                src_ref=source,
                dst_ref=faces.at[plane // 3, plane % 3, cut] if stop is None else relay.at[stop],
                send_sem=face_send.at[way, plane] if passed is None else relay_send.at[passed],
                recv_sem=face_recv.at[way, plane] if stop is None else relay_recv.at[stop],
                device_id=(group, where),
                device_id_type=MESH,
            )

        ways = (
            (0, down, has_down, has_up, 0, run_down, run - 1),
            (1, up, has_up, has_down, RUN - 1, run_up, run + RUN),
        )
        for plane in (0, 1, 2, 5, 4, 3):
            for way, where, _, _, end, crosses, _ in ways:
                for part in range(2) if (way, plane, 0) in slots_of else (None,):
                    if (way, plane, part) in slots_of:
                        at, stop = slots_of[way, plane, part]
                        pl.when(crosses & (place == end))(face_copy(way, plane, run + at, part, stop).start)
                    else:
                        pl.when(crosses & (place == end))(face_copy(way, plane, where, part).start)
        for plane in range(3 * half):
            for way, where, _, _, end, _, _ in ways:
                pl.when(place != end)(face_copy(way, plane, where).start)

        def pass_on(turn):
            for way, _, _, _, _, crosses, target in ways:
                for (relay_way, plane, part), (at, stop) in slots_of.items():
                    if relay_way == way and (plane in FIRST[way]) == (turn == 0):

                        def forward():
                            face_copy(way, plane, target, part, stop).wait_recv()
                            face_copy(way, plane, target, part, passed=stop).start()

                        pl.when(crosses & (place == at))(forward)

        for copy in small:
            copy.wait()

        zero_rows = jnp.zeros((8, cols), jnp.float32)
        for comp in range(3):
            for slot in range(slots):
                for plane in range(planes):
                    field[slot, comp, plane, rows : rows + 8, :] = zero_rows
            for slot in range(half):
                low_face[slot, comp, rows : rows + 8, :] = zero_rows
                high_face[slot, comp, rows : rows + 8, :] = zero_rows

        def clear(face_ref):
            for slot in range(half):
                for comp in range(3):
                    face_ref[slot, comp, 0:rows, :] = jnp.zeros((rows, cols), jnp.float32)

        pl.when(slab == 0)(lambda: clear(low_face))
        pl.when(slab == slabs - 1)(lambda: clear(high_face))

        coef = []
        for slot in range(slots):
            node = slot_node[slot]
            index = jnp.clip(node, 0, node_weight.shape[0] - 1)
            value = node_weight[index] * node_stiffness[index]
            coef.append(jnp.where(node < node_weight.shape[0], value, 0.0))

        last = lax.broadcasted_iota(jnp.int32, (8, cols), 1) == cols - 1
        next_rows = lax.broadcasted_iota(jnp.int32, (8, cols), 0) == 0

        def modes_of(plane_ref, block):
            def load(comp):
                return [plane_ref[comp, pl.ds(pl.multiple_of((block + k) * 8, 8), 8), :] for k in range(2)]

            return plane_modes(load, next_rows, last)

        def keep(slot, block, modes):
            for comp in range(3):
                for mode in range(4):
                    kept[slot, comp, mode, pl.ds(pl.multiple_of(block * 8, 8), 8), :] = modes[comp][mode]

        def kept_modes(slot, block):
            span = pl.ds(pl.multiple_of(block * 8, 8), 8)
            return [[kept[slot, comp, mode, span, :] for mode in range(4)] for comp in range(3)]

        for slot in range(slots):
            loads[slot].wait()

            def block_step(block, carry):
                here = modes_of(field.at[slot, :, 0], block)
                if slot >= half:
                    keep(slot, block, here)
                for layer in range(planes - 1):
                    above = modes_of(field.at[slot, :, layer + 1], block)
                    value = coef[slot] * layer_energy(here, above)
                    spot = (lax.rem(block, 2), lax.div(block, 2), layer)
                    in_sums[spot] = value if slot == 0 else in_sums[spot] + value
                    here = above
                if slot < half:
                    keep(slot, block, here)
                return carry

            lax.fori_loop(0, rows // 8, block_step, 0, unroll=2)
            if slot < 2:
                pass_on(slot)

        def swap(sums, mate_sums):
            return remote(sums.at[1 - core], mate_sums, mate)

        def spread(sums, mate_sums, pair, peer_sums):
            for index in range(chips):
                pair[index] = sums[core, index] + mate_sums[index]
            copies = []
            for k in range(1, chips):
                copies += remote(pair.at[lax.rem(chip + k, chips)], peer_sums.at[k - 1], peers[k - 1])
            return copies

        def total(pair, peer_sums, layer):
            return pair[chip, layer] + add_up([peer_sums[k, layer] for k in range(chips - 1)])

        in_swap = swap(in_sums, in_mate)
        arrive(des_planes)
        des_pad[pl.ds(2, planes), own, :] = design[...]
        des_pad[pl.ds(0, 2), own, :] = jnp.where(has_down, des_z[0], 0.0)
        des_pad[pl.ds(planes + 2, 2), own, :] = jnp.where(has_up, des_z[1], 0.0)
        for plane in range(planes + 4):
            cut_edges(des_edge, plane, des_pad, plane)
        des_rows = send_rows(des_edge, des_y)


        arrive(des_rows)
        for rim, first, cond in rims:
            des_pad[:, pl.ds(first, 2), :] = jnp.where(cond, des_y[rim], 0.0)
        row_at = lax.broadcasted_iota(jnp.int32, (tile, cols), 0) + group * tile
        ones = []
        for dy in range(3):
            within = lambda y: jnp.where((y >= 0) & (y < groups * tile), 1.0, 0.0)
            ones.append(within(row_at) if dy == 0 else within(row_at - dy) + within(row_at + dy))
        base = math.tanh(BETA * ETA)
        scale = base + math.tanh(BETA * (1.0 - ETA))
        filt_rows = [row_sums(des_pad, p) for p in range(planes + 4)]
        for plane in range(planes):
            z = slab * planes + plane
            here = lambda d: jnp.where((z + d >= 0) & (z + d < slabs * planes), 1.0, 0.0)
            gains = [1.0, here(-1) + here(1), here(-2) + here(2)]
            cover = smooth([[v * gain for v in ones] for gain in gains], cols)
            filtered = smooth(z_sums(filt_rows, plane + 2), cols) / cover
            level = jnp.tanh(BETA * (filtered - ETA))
            projected = (base + level) / scale
            slope = BETA * (1.0 - level * level) / scale
            fac[plane] = (-3.0 * (1.0 - E_FLOOR)) * (projected * projected) * slope / cover
        factor = remote(fac.at[planes - 1], fac_low, (group, up), has_up, has_down)
        arrive(in_swap)
        in_spread = spread(in_sums, in_mate, in_pair, in_peers)

        def face_energy(slot):
            for comp in range(3):
                for way, where, _, recv_if, *_ in ways:
                    pl.when(recv_if)(face_copy(way, 3 * slot + comp, where).wait_recv)

            def face_step(block, carry):
                spot = lambda layer: (lax.rem(block, 2), lax.div(block, 2), layer)
                lower = layer_energy(modes_of(low_face.at[slot], block), kept_modes(half + slot, block))
                value = coef[half + slot] * lower
                face_sums[spot(0)] = value if slot == 0 else face_sums[spot(0)] + value
                upper = layer_energy(kept_modes(slot, block), modes_of(high_face.at[slot], block))
                value = coef[slot] * upper
                face_sums[spot(1)] = value if slot == 0 else face_sums[spot(1)] + value
                return carry

            lax.fori_loop(0, rows // 8, face_step, 0, unroll=4)

        def top_energy():
            def top_step(block, carry):
                spot = (lax.rem(block, 2), lax.div(block, 2), 1)
                zero = jnp.zeros((8, cols), jnp.float32)
                for slot in range(half, slots):
                    modes = modes_of(field.at[slot, :, planes - 1], block)
                    face_sums[spot] += coef[slot] * layer_energy(modes, [(zero,) * 4] * 3)
                return carry

            lax.fori_loop(0, rows // 8, top_step, 0)

        face_energy(0)
        pl.when(slab == slabs - 1)(top_energy)

        for slot in range(1, half):
            face_energy(slot)
        face_swap = swap(face_sums, face_mate)

        def corners(edge, lower, upper, dst):
            copies = []
            for rim, step, send_if, recv_if in ((0, -1, has_prev, has_next), (1, 1, has_next, has_prev)):
                for part, side, where, send_s, recv_s in (
                    (lower, 1, down, has_down, has_up),
                    (upper, 0, up, has_up, has_down),
                ):
                    copies += remote(
                        edge.at[rim, part], dst[side].at[rim], (group + step, where), send_if & send_s, recv_if & recv_s
                    )
            return copies

        arrive(in_spread)
        inner = planes - 1
        for layer in range(inner):
            sen[layer] = total(in_pair, in_peers, layer) * fac[layer]
        sen_edge[0, 0:inner] = sen[:, 0:2, :]
        sen_edge[1, 0:inner] = sen[:, tile - 2 : tile, :]
        halo = send_z(sen.at[pl.ds(0, 2)], sen_high, sen.at[inner - 1], sen_low)
        halo += corners(sen_edge, pl.ds(0, 2), inner - 1, (sen_cl, sen_ch))

        arrive(face_swap)
        face_spread = spread(face_sums, face_mate, face_pair, face_peers)
        sen_pad[pl.ds(2, inner), own, :] = sen[...]
        arrive(factor)
        arrive(face_spread)
        late[0] = total(face_pair, face_peers, 0) * jnp.where(has_down, fac_low[...], 0.0)
        late[1] = total(face_pair, face_peers, 1) * fac[inner]
        late_halo = send_z(late.at[0], late_z.at[1], late.at[1], late_z.at[0])
        sen_edge[0, inner : inner + 2] = late[:, 0:2, :]
        sen_edge[1, inner : inner + 2] = late[:, tile - 2 : tile, :]
        late_halo += corners(sen_edge, inner, inner + 1, (late_c.at[0], late_c.at[1]))
        late_halo += send_rows(sen_edge, sen_y)

        arrive(halo)
        sen_pad[0, own, :] = jnp.where(has_down, sen_low[...], 0.0)
        sen_pad[pl.ds(planes + 2, 2), own, :] = jnp.where(has_up, sen_high[...], 0.0)
        for rim, first, cond in rims:
            span = pl.ds(first, 2)
            sen_pad[0, span, :] = jnp.where(cond & has_down, sen_cl[rim], 0.0)
            sen_pad[pl.ds(planes + 2, 2), span, :] = jnp.where(cond & has_up, sen_ch[rim], 0.0)
        arrive(late_halo)
        sen_pad[1, own, :] = jnp.where(has_down, late[0] + late_z[0], 0.0)
        sen_pad[planes + 1, own, :] = late[1] + jnp.where(has_up, late_z[1], 0.0)
        for rim, first, cond in rims:
            span = pl.ds(first, 2)
            sen_pad[1, span, :] = jnp.where(cond & has_down, sen_y[rim, inner] + late_c[0, rim], 0.0)
            sen_pad[pl.ds(2, inner), span, :] = jnp.where(cond, sen_y[rim, 0:inner], 0.0)
            sen_pad[planes + 1, span, :] = jnp.where(cond, sen_y[rim, inner + 1], 0.0) + jnp.where(
                cond & has_up, late_c[1, rim], 0.0
            )
        sens_rows = [row_sums(sen_pad, p) for p in range(planes + 4)]
        for plane in range(planes):
            out[plane] = smooth(z_sums(sens_rows, plane + 2), cols)

        for copy, send_if, _ in started:
            when(send_if, copy.wait_send)
        for plane in range(3 * half):
            for way, where, send_if, *_ in ways:
                pl.when(send_if)(face_copy(way, plane, where).wait_send)
        for way, where, _, _, _, crosses, _ in ways:
            for (relay_way, plane, part), (at, stop) in slots_of.items():
                if relay_way == way:
                    pl.when(crosses & (place == at))(face_copy(way, plane, where, part, passed=stop).wait_send)

    vmem = lambda *shape: pltpu.VMEM(shape, jnp.float32)
    copies = 2 + 2 + 1 + 2 * chips + 6 + 8
    inner = planes - 1
    scratch = [
        pltpu.SMEM((slots,), jnp.int32),
        pltpu.SMEM((nodes,), jnp.float32),
        pltpu.SMEM((nodes,), jnp.float32),
        vmem(planes, tile, cols),
        vmem(slots, 3, planes, rows + 8, cols),
        vmem(slots, 3, 4, rows, cols),
        vmem(half, 3, rows + 8, cols),
        vmem(half, 3, rows + 8, cols),
        vmem(stops, rows // 2, cols),
        vmem(planes + 4, 24, cols),
        vmem(2, 2, tile, cols),
        vmem(2, planes + 4, 2, cols),
        vmem(2, planes + 4, 2, cols),
        vmem(planes, tile, cols),
        vmem(tile, cols),
        vmem(2, chips, inner, tile, cols),
        vmem(chips, inner, tile, cols),
        vmem(chips, inner, tile, cols),
        vmem(chips - 1, inner, tile, cols),
        vmem(inner, tile, cols),
        vmem(planes + 4, 24, cols),
        vmem(tile, cols),
        vmem(2, tile, cols),
        vmem(2, 2, cols),
        vmem(2, 2, 2, cols),
        vmem(2, planes + 1, 2, cols),
        vmem(2, planes + 1, 2, cols),
        vmem(2, chips, 2, tile, cols),
        vmem(chips, 2, tile, cols),
        vmem(chips, 2, tile, cols),
        vmem(chips - 1, 2, tile, cols),
        vmem(2, tile, cols),
        vmem(2, tile, cols),
        vmem(2, 2, 2, cols),
        pltpu.SemaphoreType.DMA((slots,)),
        pltpu.SemaphoreType.DMA((4,)),
        pltpu.SemaphoreType.DMA((copies,)),
        pltpu.SemaphoreType.DMA((copies,)),
        pltpu.SemaphoreType.DMA((2, 3 * half)),
        pltpu.SemaphoreType.DMA((2, 3 * half)),
        pltpu.SemaphoreType.DMA((stops,)),
        pltpu.SemaphoreType.DMA((stops,)),
    ]
    return kernel, scratch


def solution(mesh):
    groups, slabs = mesh.shape["nodes"], mesh.shape["space"]

    def per_device(displacement, slot_node, node_weight, node_stiffness, design):
        slots, _, planes, rows, cols = displacement.shape
        kernel, scratch = make_kernel(groups, slabs, node_weight.shape[0], slots, planes, rows, cols, design.shape[1])
        return pl.pallas_call(
            kernel,
            out_shape=jax.ShapeDtypeStruct(design.shape, jnp.float32),
            in_specs=[pl.BlockSpec(memory_space=pltpu.HBM)] * 5,
            out_specs=pl.BlockSpec(memory_space=pltpu.VMEM),
            scratch_shapes=scratch,
            compiler_params=pltpu.CompilerParams(
                collective_id=0, has_side_effects=True, vmem_limit_bytes=60 * 2**20
            ),
            cost_estimate=pl.CostEstimate(flops=40_000_000, bytes_accessed=4_000_000, transcendentals=8192),
            name="sensitivity",
        )(displacement, slot_node, node_weight, node_stiffness, design)

    return jax.shard_map(
        per_device,
        mesh=mesh,
        in_specs=(
            P("nodes", None, "space", None, None),
            P("nodes"),
            P(),
            P(),
            P("space", "nodes", None),
        ),
        out_specs=P("space", "nodes", None),
        check_vma=False,
    )
```

```python
import math

import jax
import jax.numpy as jnp
from jax import lax
from jax.experimental import pallas as pl
from jax.experimental.pallas import tpu as pltpu
from jax.sharding import PartitionSpec as P

POISSON = 0.3
E_FLOOR = 0.001
BETA = 8.0
ETA = 0.5
RADIUS = 2.5
MESH = pl.DeviceIdType.MESH
RUN = 4
RELAY_DOWN = {(1, 0): 3, (1, 1): 3, (4, 0): 1, (4, 1): 2, (2, 0): 1, (2, 1): 1, (5, 0): 2, (5, 1): 2}
RELAY_UP = {(1, 0): 0, (1, 1): 0, (4, 0): 0, (4, 1): 1, (2, 0): 2, (2, 1): 2, (5, 0): 1, (5, 1): 1}
FIRST = ({1, 2, 5}, {1})


def relay_slots():
    used, slots = {}, {}
    for way, relays in enumerate((RELAY_DOWN, RELAY_UP)):
        for (plane, part), at in relays.items():
            slots[way, plane, part] = (at, used.get(at, 0))
            used[at] = used.get(at, 0) + 1
    return slots, max(used.values())


def weight(dz, dy, dx):
    return max(0.0, RADIUS - math.sqrt(dz * dz + dy * dy + dx * dx))


def add_up(terms):
    total = None
    for term in terms:
        total = term if total is None else total + term
    return total


def next_lane(v, last):
    return jnp.where(last, 0.0, pltpu.roll(v, v.shape[1] - 1, 1))


def plane_modes(load, next_rows, last):
    modes = []
    for comp in range(3):
        here, below = load(comp)
        up = pltpu.roll(jnp.where(next_rows, below, here), 7, 0)
        ysum, ydif = up + here, up - here
        ysum_x, ydif_x = next_lane(ysum, last), next_lane(ydif, last)
        modes.append((ysum_x + ysum, ysum_x - ysum, ydif_x + ydif, ydif_x - ydif))
    return modes


def layer_energy(low, high):
    lam = POISSON / ((1.0 + POISSON) * (1.0 - 2.0 * POISSON))
    shear = 1.0 / (2.0 * (1.0 + POISSON))
    sums = [[lo + hi for lo, hi in zip(a, b)] for a, b in zip(low, high)]
    difs = [[hi - lo for lo, hi in zip(a, b)] for a, b in zip(low, high)]
    (_, ax, ay, axy), (_, bx, by, bxy), (_, cx, cy, cxy) = sums
    (az, azx, ayz, axyz), (bz, bzx, byz, bxyz), (cz, czx, cyz, cxyz) = difs
    sq = lambda v: v * v
    div = sq(ax + by + cz)
    diag = sq(ax) + sq(by) + sq(cz)
    skew = sq(ay + bx) + sq(az + cx) + sq(bz + cy)
    even = sq(bxy + czx) + sq(axy + cyz) + sq(azx + byz)
    odd = sq(bxy - czx) + sq(axy - cyz) + sq(azx - byz)
    mixed = sq(ayz + bzx) + sq(ayz + cxy) + sq(bzx + cxy)
    high_order = sq(axyz) + sq(bxyz) + sq(cxyz)
    return (
        (lam / 16.0) * div
        + (2.0 * shear / 16.0) * diag
        + (shear / 16.0) * skew
        + ((lam + 1.5 * shear) / 48.0) * even
        + (1.5 * shear / 48.0) * odd
        + (shear / 48.0) * mixed
        + ((lam + 4.0 * shear) / 144.0) * high_order
    )


def smooth(windows, cols):
    lanes = lax.broadcasted_iota(jnp.int32, windows[0][0].shape, 1)
    total = None
    for dx in range(3):
        part = add_up(
            [weight(i, j, dx) * windows[i][j] for i in range(3) for j in range(3) if weight(i, j, dx) > 0.0]
        )
        if dx > 0:
            right = jnp.where(lanes < cols - dx, pltpu.roll(part, cols - dx, 1), 0.0)
            left = jnp.where(lanes >= dx, pltpu.roll(part, dx, 1), 0.0)
            part = left + right
        total = part if total is None else total + part
    return total


def row_sums(field, plane):
    at = lambda first: field[plane, first : first + 8, :]
    return [at(8), at(7) + at(9), at(6) + at(10)]


def z_sums(rows, plane):
    return [
        rows[plane],
        [a + b for a, b in zip(rows[plane - 1], rows[plane + 1])],
        [a + b for a, b in zip(rows[plane - 2], rows[plane + 2])],
    ]


def make_kernel(groups, slabs, nodes, slots, planes, rows, cols, tile):
    half = slots // 2
    chips = groups // 2
    slots_of, stops = relay_slots()

    def kernel(
        disp, slot_node_in, node_weight_in, node_stiffness_in, design_in, out,
        slot_node, node_weight, node_stiffness, design, field, kept, low_face, high_face, relay,
        des_pad, des_z, des_edge, des_y, fac, fac_low,
        in_sums, in_mate, in_pair, in_peers, sen, sen_pad, sen_low, sen_high, sen_cl, sen_ch, sen_edge, sen_y,
        face_sums, face_mate, face_pair, face_peers, late, late_z, late_c,
        load_sem, small_sem, send_sem, recv_sem, face_send, face_recv, relay_send, relay_recv,
    ):
        group = lax.axis_index("nodes")
        slab = lax.axis_index("space")
        core = lax.rem(group, 2)
        chip = lax.div(group, 2)
        place = lax.rem(slab, RUN)
        run = slab - place
        down, up = slab - 1, slab + 1
        has_prev, has_next = group > 0, group < groups - 1
        has_down, has_up = slab > 0, slab < slabs - 1
        run_down, run_up = run > 0, run < slabs - RUN
        mate = (group + 1 - 2 * core, slab)
        peers = [(2 * lax.rem(chip + k, chips) + core, slab) for k in range(1, chips)]

        def when(condition, action):
            if condition is None:
                action()
            else:
                pl.when(condition)(action)

        aside = group + 2 * core - 1
        partners = [((group, down), run_down & (place == 0)), ((group, up), run_up & (place == RUN - 1))]
        partners += [((group, run + lax.rem(place + k, RUN)), None) for k in range(1, RUN)]
        partners += [(mate, None)] + [(peer, None) for peer in peers]
        partners.append(((aside, slab), (aside >= 0) & (aside < groups)))
        barrier = pltpu.get_barrier_semaphore()
        for device, cond in partners:
            when(cond, lambda: pl.semaphore_signal(barrier, inc=1, device_id=device, device_id_type=MESH))
        loads = []
        for slot in range(slots):
            load = pltpu.make_async_copy(
                disp.at[slot], field.at[slot, :, :, pl.ds(0, rows), :], load_sem.at[slot]
            )
            load.start()
            loads.append(load)
        small = []
        for number, (source, target) in enumerate(
            (
                (design_in, design),
                (slot_node_in, slot_node),
                (node_weight_in, node_weight),
                (node_stiffness_in, node_stiffness),
            )
        ):
            small.append(pltpu.make_async_copy(source, target, small_sem.at[number]))
            small[-1].start()
        pl.semaphore_wait(barrier, sum(1 if cond is None else cond.astype(jnp.int32) for _, cond in partners))

        started = []

        def remote(src, dst, device, send_if=None, recv_if=None):
            number = len(started)
            copy = pltpu.make_async_remote_copy(
                src_ref=src, dst_ref=dst, send_sem=send_sem.at[number], recv_sem=recv_sem.at[number],
                device_id=device, device_id_type=MESH,
            )
            started.append((copy, send_if, recv_if))
            when(send_if, copy.start)
            return started[-1:]

        def arrive(copies):
            for copy, _, recv_if in copies:
                when(recv_if, copy.wait_recv)

        def send_z(below_src, below_dst, above_src, above_dst):
            return remote(below_src, below_dst, (group, down), has_down, has_up) + remote(
                above_src, above_dst, (group, up), has_up, has_down
            )

        def send_rows(edge, dst):
            return remote(edge.at[0], dst.at[0], (group - 1, slab), has_prev, has_next) + remote(
                edge.at[1], dst.at[1], (group + 1, slab), has_next, has_prev
            )

        rims = ((0, 16, has_next), (1, 6, has_prev))
        own = pl.ds(8, tile)
        cut_edges = lambda edge, at, pad_ref, plane: (
            edge.__setitem__((0, at), pad_ref[plane, 8:10, :]),
            edge.__setitem__((1, at), pad_ref[plane, tile + 6 : tile + 8, :]),
        )

        des_planes = send_z(
            design_in.at[pl.ds(0, 2)], des_z.at[1], design_in.at[pl.ds(planes - 2, 2)], des_z.at[0]
        )

        def face_copy(way, plane, where, part=None, stop=None, passed=None):
            cut = pl.ds(0, rows) if part is None else pl.ds(part * (rows // 2), rows // 2)
            if passed is not None:
                source = relay.at[passed]
            elif way == 0:
                source = disp.at[plane // 3, plane % 3, 0, cut]
            else:
                source = disp.at[half + plane // 3, plane % 3, planes - 1, cut]
            faces = (high_face, low_face)[way]
            return pltpu.make_async_remote_copy(
                src_ref=source,
                dst_ref=faces.at[plane // 3, plane % 3, cut] if stop is None else relay.at[stop],
                send_sem=face_send.at[way, plane // 3] if passed is None else relay_send.at[passed],
                recv_sem=face_recv.at[way, plane // 3] if stop is None else relay_recv.at[stop],
                device_id=(group, where),
                device_id_type=MESH,
            )

        def slot_copy(way, slot, where):
            return pltpu.make_async_remote_copy(
                src_ref=disp.at[slot, :, 0] if way == 0 else disp.at[half + slot, :, planes - 1],
                dst_ref=(high_face, low_face)[way].at[slot, :, pl.ds(0, rows)],
                send_sem=face_send.at[way, slot],
                recv_sem=face_recv.at[way, slot],
                device_id=(group, where),
                device_id_type=MESH,
            )

        ways = (
            (0, down, has_down, has_up, 0, run_down, run - 1),
            (1, up, has_up, has_down, RUN - 1, run_up, run + RUN),
        )
        for plane in (0, 1, 2, 5, 4, 3):
            for way, where, _, _, end, crosses, _ in ways:
                for part in range(2) if (way, plane, 0) in slots_of else (None,):
                    if (way, plane, part) in slots_of:
                        at, stop = slots_of[way, plane, part]
                        pl.when(crosses & (place == end))(face_copy(way, plane, run + at, part, stop).start)
                    else:
                        pl.when(crosses & (place == end))(face_copy(way, plane, where, part).start)
        for slot in range(half):
            for way, where, _, _, end, _, _ in ways:
                pl.when(place != end)(slot_copy(way, slot, where).start)

        def pass_on(turn):
            for way, _, _, _, _, crosses, target in ways:
                for (relay_way, plane, part), (at, stop) in slots_of.items():
                    if relay_way == way and (plane in FIRST[way]) == (turn == 0):

                        def forward():
                            face_copy(way, plane, target, part, stop).wait_recv()
                            face_copy(way, plane, target, part, passed=stop).start()

                        pl.when(crosses & (place == at))(forward)

        for copy in small:
            copy.wait()

        zero_rows = jnp.zeros((8, cols), jnp.float32)
        for comp in range(3):
            for slot in range(slots):
                for plane in range(planes):
                    field[slot, comp, plane, rows : rows + 8, :] = zero_rows
            for slot in range(half):
                low_face[slot, comp, rows : rows + 8, :] = zero_rows
                high_face[slot, comp, rows : rows + 8, :] = zero_rows

        def clear(face_ref):
            for slot in range(half):
                for comp in range(3):
                    face_ref[slot, comp, 0:rows, :] = jnp.zeros((rows, cols), jnp.float32)

        pl.when(slab == 0)(lambda: clear(low_face))
        pl.when(slab == slabs - 1)(lambda: clear(high_face))

        coef = []
        for slot in range(slots):
            node = slot_node[slot]
            index = jnp.clip(node, 0, node_weight.shape[0] - 1)
            value = node_weight[index] * node_stiffness[index]
            coef.append(jnp.where(node < node_weight.shape[0], value, 0.0))

        last = lax.broadcasted_iota(jnp.int32, (8, cols), 1) == cols - 1
        next_rows = lax.broadcasted_iota(jnp.int32, (8, cols), 0) == 0

        def modes_of(plane_ref, block):
            def load(comp):
                return [plane_ref[comp, pl.ds(pl.multiple_of((block + k) * 8, 8), 8), :] for k in range(2)]

            return plane_modes(load, next_rows, last)

        def keep(slot, block, modes):
            for comp in range(3):
                for mode in range(4):
                    kept[slot, comp, mode, pl.ds(pl.multiple_of(block * 8, 8), 8), :] = modes[comp][mode]

        def kept_modes(slot, block):
            span = pl.ds(pl.multiple_of(block * 8, 8), 8)
            return [[kept[slot, comp, mode, span, :] for mode in range(4)] for comp in range(3)]

        for slot in range(slots):
            loads[slot].wait()

            def block_step(block, carry):
                here = modes_of(field.at[slot, :, 0], block)
                if slot >= half:
                    keep(slot, block, here)
                for layer in range(planes - 1):
                    above = modes_of(field.at[slot, :, layer + 1], block)
                    value = coef[slot] * layer_energy(here, above)
                    spot = (lax.rem(block, 2), lax.div(block, 2), layer)
                    in_sums[spot] = value if slot == 0 else in_sums[spot] + value
                    here = above
                if slot < half:
                    keep(slot, block, here)
                return carry

            lax.fori_loop(0, rows // 8, block_step, 0, unroll=2)
            if slot < 2:
                pass_on(slot)

        def swap(sums, mate_sums):
            return remote(sums.at[1 - core], mate_sums, mate)

        def spread(sums, mate_sums, pair, peer_sums):
            for index in range(chips):
                pair[index] = sums[core, index] + mate_sums[index]
            copies = []
            for k in range(1, chips):
                copies += remote(pair.at[lax.rem(chip + k, chips)], peer_sums.at[k - 1], peers[k - 1])
            return copies

        def total(pair, peer_sums, layer):
            return pair[chip, layer] + add_up([peer_sums[k, layer] for k in range(chips - 1)])

        in_swap = swap(in_sums, in_mate)
        arrive(des_planes)
        des_pad[pl.ds(2, planes), own, :] = design[...]
        des_pad[pl.ds(0, 2), own, :] = jnp.where(has_down, des_z[0], 0.0)
        des_pad[pl.ds(planes + 2, 2), own, :] = jnp.where(has_up, des_z[1], 0.0)
        for plane in range(planes + 4):
            cut_edges(des_edge, plane, des_pad, plane)
        des_rows = send_rows(des_edge, des_y)


        arrive(des_rows)
        for rim, first, cond in rims:
            des_pad[:, pl.ds(first, 2), :] = jnp.where(cond, des_y[rim], 0.0)
        row_at = lax.broadcasted_iota(jnp.int32, (tile, cols), 0) + group * tile
        ones = []
        for dy in range(3):
            within = lambda y: jnp.where((y >= 0) & (y < groups * tile), 1.0, 0.0)
            ones.append(within(row_at) if dy == 0 else within(row_at - dy) + within(row_at + dy))
        base = math.tanh(BETA * ETA)
        scale = base + math.tanh(BETA * (1.0 - ETA))
        filt_rows = [row_sums(des_pad, p) for p in range(planes + 4)]
        for plane in range(planes):
            z = slab * planes + plane
            here = lambda d: jnp.where((z + d >= 0) & (z + d < slabs * planes), 1.0, 0.0)
            gains = [1.0, here(-1) + here(1), here(-2) + here(2)]
            cover = smooth([[v * gain for v in ones] for gain in gains], cols)
            filtered = smooth(z_sums(filt_rows, plane + 2), cols) / cover
            level = jnp.tanh(BETA * (filtered - ETA))
            projected = (base + level) / scale
            slope = BETA * (1.0 - level * level) / scale
            fac[plane] = (-3.0 * (1.0 - E_FLOOR)) * (projected * projected) * slope / cover
        factor = remote(fac.at[planes - 1], fac_low, (group, up), has_up, has_down)
        arrive(in_swap)
        in_spread = spread(in_sums, in_mate, in_pair, in_peers)

        def face_energy(slot):
            for way, where, _, recv_if, *_ in ways:
                pl.when(recv_if)(slot_copy(way, slot, where).wait_recv)

            def face_step(block, carry):
                spot = lambda layer: (lax.rem(block, 2), lax.div(block, 2), layer)
                lower = layer_energy(modes_of(low_face.at[slot], block), kept_modes(half + slot, block))
                value = coef[half + slot] * lower
                face_sums[spot(0)] = value if slot == 0 else face_sums[spot(0)] + value
                upper = layer_energy(kept_modes(slot, block), modes_of(high_face.at[slot], block))
                value = coef[slot] * upper
                face_sums[spot(1)] = value if slot == 0 else face_sums[spot(1)] + value
                return carry

            lax.fori_loop(0, rows // 8, face_step, 0, unroll=4)

        def top_energy():
            def top_step(block, carry):
                spot = (lax.rem(block, 2), lax.div(block, 2), 1)
                zero = jnp.zeros((8, cols), jnp.float32)
                for slot in range(half, slots):
                    modes = modes_of(field.at[slot, :, planes - 1], block)
                    face_sums[spot] += coef[slot] * layer_energy(modes, [(zero,) * 4] * 3)
                return carry

            lax.fori_loop(0, rows // 8, top_step, 0)

        face_energy(0)
        pl.when(slab == slabs - 1)(top_energy)

        for slot in range(1, half):
            face_energy(slot)
        face_swap = swap(face_sums, face_mate)

        def corners(edge, lower, upper, dst):
            copies = []
            for rim, step, send_if, recv_if in ((0, -1, has_prev, has_next), (1, 1, has_next, has_prev)):
                for part, side, where, send_s, recv_s in (
                    (lower, 1, down, has_down, has_up),
                    (upper, 0, up, has_up, has_down),
                ):
                    copies += remote(
                        edge.at[rim, part], dst[side].at[rim], (group + step, where), send_if & send_s, recv_if & recv_s
                    )
            return copies

        arrive(in_spread)
        inner = planes - 1
        for layer in range(inner):
            sen[layer] = total(in_pair, in_peers, layer) * fac[layer]
        sen_edge[0, 0:inner] = sen[:, 0:2, :]
        sen_edge[1, 0:inner] = sen[:, tile - 2 : tile, :]
        halo = send_z(sen.at[pl.ds(0, 2)], sen_high, sen.at[inner - 1], sen_low)
        halo += corners(sen_edge, pl.ds(0, 2), inner - 1, (sen_cl, sen_ch))

        arrive(face_swap)
        face_spread = spread(face_sums, face_mate, face_pair, face_peers)
        sen_pad[pl.ds(2, inner), own, :] = sen[...]
        arrive(factor)
        arrive(face_spread)
        late[0] = total(face_pair, face_peers, 0) * jnp.where(has_down, fac_low[...], 0.0)
        late[1] = total(face_pair, face_peers, 1) * fac[inner]
        late_halo = send_z(late.at[0], late_z.at[1], late.at[1], late_z.at[0])
        sen_edge[0, inner : inner + 2] = late[:, 0:2, :]
        sen_edge[1, inner : inner + 2] = late[:, tile - 2 : tile, :]
        late_halo += corners(sen_edge, inner, inner + 1, (late_c.at[0], late_c.at[1]))
        late_halo += send_rows(sen_edge, sen_y)

        arrive(halo)
        sen_pad[0, own, :] = jnp.where(has_down, sen_low[...], 0.0)
        sen_pad[pl.ds(planes + 2, 2), own, :] = jnp.where(has_up, sen_high[...], 0.0)
        for rim, first, cond in rims:
            span = pl.ds(first, 2)
            sen_pad[0, span, :] = jnp.where(cond & has_down, sen_cl[rim], 0.0)
            sen_pad[pl.ds(planes + 2, 2), span, :] = jnp.where(cond & has_up, sen_ch[rim], 0.0)
        arrive(late_halo)
        sen_pad[1, own, :] = jnp.where(has_down, late[0] + late_z[0], 0.0)
        sen_pad[planes + 1, own, :] = late[1] + jnp.where(has_up, late_z[1], 0.0)
        for rim, first, cond in rims:
            span = pl.ds(first, 2)
            sen_pad[1, span, :] = jnp.where(cond & has_down, sen_y[rim, inner] + late_c[0, rim], 0.0)
            sen_pad[pl.ds(2, inner), span, :] = jnp.where(cond, sen_y[rim, 0:inner], 0.0)
            sen_pad[planes + 1, span, :] = jnp.where(cond, sen_y[rim, inner + 1], 0.0) + jnp.where(
                cond & has_up, late_c[1, rim], 0.0
            )
        sens_rows = [row_sums(sen_pad, p) for p in range(planes + 4)]
        for plane in range(planes):
            out[plane] = smooth(z_sums(sens_rows, plane + 2), cols)

        for copy, send_if, _ in started:
            when(send_if, copy.wait_send)
        for slot in range(half):
            for way, where, send_if, *_ in ways:
                pl.when(send_if)(slot_copy(way, slot, where).wait_send)
        for way, where, _, _, _, crosses, _ in ways:
            for (relay_way, plane, part), (at, stop) in slots_of.items():
                if relay_way == way:
                    pl.when(crosses & (place == at))(face_copy(way, plane, where, part, passed=stop).wait_send)

    vmem = lambda *shape: pltpu.VMEM(shape, jnp.float32)
    copies = 2 + 2 + 1 + 2 * chips + 6 + 8
    inner = planes - 1
    scratch = [
        pltpu.SMEM((slots,), jnp.int32),
        pltpu.SMEM((nodes,), jnp.float32),
        pltpu.SMEM((nodes,), jnp.float32),
        vmem(planes, tile, cols),
        vmem(slots, 3, planes, rows + 8, cols),
        vmem(slots, 3, 4, rows, cols),
        vmem(half, 3, rows + 8, cols),
        vmem(half, 3, rows + 8, cols),
        vmem(stops, rows // 2, cols),
        vmem(planes + 4, 24, cols),
        vmem(2, 2, tile, cols),
        vmem(2, planes + 4, 2, cols),
        vmem(2, planes + 4, 2, cols),
        vmem(planes, tile, cols),
        vmem(tile, cols),
        vmem(2, chips, inner, tile, cols),
        vmem(chips, inner, tile, cols),
        vmem(chips, inner, tile, cols),
        vmem(chips - 1, inner, tile, cols),
        vmem(inner, tile, cols),
        vmem(planes + 4, 24, cols),
        vmem(tile, cols),
        vmem(2, tile, cols),
        vmem(2, 2, cols),
        vmem(2, 2, 2, cols),
        vmem(2, planes + 1, 2, cols),
        vmem(2, planes + 1, 2, cols),
        vmem(2, chips, 2, tile, cols),
        vmem(chips, 2, tile, cols),
        vmem(chips, 2, tile, cols),
        vmem(chips - 1, 2, tile, cols),
        vmem(2, tile, cols),
        vmem(2, tile, cols),
        vmem(2, 2, 2, cols),
        pltpu.SemaphoreType.DMA((slots,)),
        pltpu.SemaphoreType.DMA((4,)),
        pltpu.SemaphoreType.DMA((copies,)),
        pltpu.SemaphoreType.DMA((copies,)),
        pltpu.SemaphoreType.DMA((2, half)),
        pltpu.SemaphoreType.DMA((2, half)),
        pltpu.SemaphoreType.DMA((stops,)),
        pltpu.SemaphoreType.DMA((stops,)),
    ]
    return kernel, scratch


def solution(mesh):
    groups, slabs = mesh.shape["nodes"], mesh.shape["space"]

    def per_device(displacement, slot_node, node_weight, node_stiffness, design):
        slots, _, planes, rows, cols = displacement.shape
        kernel, scratch = make_kernel(groups, slabs, node_weight.shape[0], slots, planes, rows, cols, design.shape[1])
        return pl.pallas_call(
            kernel,
            out_shape=jax.ShapeDtypeStruct(design.shape, jnp.float32),
            in_specs=[pl.BlockSpec(memory_space=pltpu.HBM)] * 5,
            out_specs=pl.BlockSpec(memory_space=pltpu.VMEM),
            scratch_shapes=scratch,
            compiler_params=pltpu.CompilerParams(
                collective_id=0, has_side_effects=True, vmem_limit_bytes=60 * 2**20
            ),
            cost_estimate=pl.CostEstimate(flops=40_000_000, bytes_accessed=4_000_000, transcendentals=8192),
            name="sensitivity",
        )(displacement, slot_node, node_weight, node_stiffness, design)

    return jax.shard_map(
        per_device,
        mesh=mesh,
        in_specs=(
            P("nodes", None, "space", None, None),
            P("nodes"),
            P(),
            P(),
            P("space", "nodes", None),
        ),
        out_specs=P("space", "nodes", None),
        check_vma=False,
    )
```

```python
import math

import jax
import jax.numpy as jnp
from jax import lax
from jax.experimental import pallas as pl
from jax.experimental.pallas import tpu as pltpu
from jax.sharding import PartitionSpec as P

POISSON = 0.3
E_FLOOR = 0.001
BETA = 8.0
ETA = 0.5
RADIUS = 2.5
MESH = pl.DeviceIdType.MESH
RUN = 4
RELAY_DOWN = {(1, 0): 3, (1, 1): 3, (4, 0): 1, (3, 1): 3, (4, 1): 2, (2, 0): 1, (2, 1): 1, (5, 0): 2, (5, 1): 2}
RELAY_UP = {(1, 0): 0, (1, 1): 0, (4, 0): 0, (4, 1): 1, (2, 0): 2, (2, 1): 2, (5, 0): 1, (5, 1): 1}
FIRST = ({1, 2, 5}, {1})


def relay_slots():
    used, slots = {}, {}
    for way, relays in enumerate((RELAY_DOWN, RELAY_UP)):
        for (plane, part), at in relays.items():
            slots[way, plane, part] = (at, used.get(at, 0))
            used[at] = used.get(at, 0) + 1
    return slots, max(used.values())


def weight(dz, dy, dx):
    return max(0.0, RADIUS - math.sqrt(dz * dz + dy * dy + dx * dx))


def add_up(terms):
    total = None
    for term in terms:
        total = term if total is None else total + term
    return total


def next_lane(v, last):
    return jnp.where(last, 0.0, pltpu.roll(v, v.shape[1] - 1, 1))


def plane_modes(load, next_rows, last):
    modes = []
    for comp in range(3):
        here, below = load(comp)
        up = pltpu.roll(jnp.where(next_rows, below, here), 7, 0)
        ysum, ydif = up + here, up - here
        ysum_x, ydif_x = next_lane(ysum, last), next_lane(ydif, last)
        modes.append((ysum_x + ysum, ysum_x - ysum, ydif_x + ydif, ydif_x - ydif))
    return modes


def layer_energy(low, high):
    lam = POISSON / ((1.0 + POISSON) * (1.0 - 2.0 * POISSON))
    shear = 1.0 / (2.0 * (1.0 + POISSON))
    sums = [[lo + hi for lo, hi in zip(a, b)] for a, b in zip(low, high)]
    difs = [[hi - lo for lo, hi in zip(a, b)] for a, b in zip(low, high)]
    (_, ax, ay, axy), (_, bx, by, bxy), (_, cx, cy, cxy) = sums
    (az, azx, ayz, axyz), (bz, bzx, byz, bxyz), (cz, czx, cyz, cxyz) = difs
    sq = lambda v: v * v
    div = sq(ax + by + cz)
    diag = sq(ax) + sq(by) + sq(cz)
    skew = sq(ay + bx) + sq(az + cx) + sq(bz + cy)
    even = sq(bxy + czx) + sq(axy + cyz) + sq(azx + byz)
    odd = sq(bxy - czx) + sq(axy - cyz) + sq(azx - byz)
    mixed = sq(ayz + bzx) + sq(ayz + cxy) + sq(bzx + cxy)
    high_order = sq(axyz) + sq(bxyz) + sq(cxyz)
    return (
        (lam / 16.0) * div
        + (2.0 * shear / 16.0) * diag
        + (shear / 16.0) * skew
        + ((lam + 1.5 * shear) / 48.0) * even
        + (1.5 * shear / 48.0) * odd
        + (shear / 48.0) * mixed
        + ((lam + 4.0 * shear) / 144.0) * high_order
    )


def smooth(windows, cols):
    lanes = lax.broadcasted_iota(jnp.int32, windows[0][0].shape, 1)
    total = None
    for dx in range(3):
        part = add_up(
            [weight(i, j, dx) * windows[i][j] for i in range(3) for j in range(3) if weight(i, j, dx) > 0.0]
        )
        if dx > 0:
            right = jnp.where(lanes < cols - dx, pltpu.roll(part, cols - dx, 1), 0.0)
            left = jnp.where(lanes >= dx, pltpu.roll(part, dx, 1), 0.0)
            part = left + right
        total = part if total is None else total + part
    return total


def row_sums(field, plane):
    at = lambda first: field[plane, first : first + 8, :]
    return [at(8), at(7) + at(9), at(6) + at(10)]


def z_sums(rows, plane):
    return [
        rows[plane],
        [a + b for a, b in zip(rows[plane - 1], rows[plane + 1])],
        [a + b for a, b in zip(rows[plane - 2], rows[plane + 2])],
    ]


def make_kernel(groups, slabs, nodes, slots, planes, rows, cols, tile):
    half = slots // 2
    chips = groups // 2
    slots_of, stops = relay_slots()

    def kernel(
        disp, slot_node_in, node_weight_in, node_stiffness_in, design_in, out,
        slot_node, node_weight, node_stiffness, design, field, kept, low_face, high_face, relay,
        des_pad, des_z, des_edge, des_y, fac, fac_low,
        in_sums, in_mate, in_pair, in_peers, sen, sen_pad, sen_low, sen_high, sen_cl, sen_ch, sen_edge, sen_y,
        face_sums, face_mate, face_pair, face_peers, late, late_z, late_c,
        load_sem, small_sem, send_sem, recv_sem, face_send, face_recv, relay_send, relay_recv,
    ):
        group = lax.axis_index("nodes")
        slab = lax.axis_index("space")
        core = lax.rem(group, 2)
        chip = lax.div(group, 2)
        place = lax.rem(slab, RUN)
        run = slab - place
        down, up = slab - 1, slab + 1
        has_prev, has_next = group > 0, group < groups - 1
        has_down, has_up = slab > 0, slab < slabs - 1
        run_down, run_up = run > 0, run < slabs - RUN
        mate = (group + 1 - 2 * core, slab)
        peers = [(2 * lax.rem(chip + k, chips) + core, slab) for k in range(1, chips)]

        def when(condition, action):
            if condition is None:
                action()
            else:
                pl.when(condition)(action)

        aside = group + 2 * core - 1
        partners = [((group, down), run_down & (place == 0)), ((group, up), run_up & (place == RUN - 1))]
        partners += [((group, run + lax.rem(place + k, RUN)), None) for k in range(1, RUN)]
        partners += [(mate, None)] + [(peer, None) for peer in peers]
        partners.append(((aside, slab), (aside >= 0) & (aside < groups)))
        barrier = pltpu.get_barrier_semaphore()
        for device, cond in partners:
            when(cond, lambda: pl.semaphore_signal(barrier, inc=1, device_id=device, device_id_type=MESH))
        loads = []
        for slot in range(slots):
            load = pltpu.make_async_copy(
                disp.at[slot], field.at[slot, :, :, pl.ds(0, rows), :], load_sem.at[slot]
            )
            load.start()
            loads.append(load)
        small = []
        for number, (source, target) in enumerate(
            (
                (design_in, design),
                (slot_node_in, slot_node),
                (node_weight_in, node_weight),
                (node_stiffness_in, node_stiffness),
            )
        ):
            small.append(pltpu.make_async_copy(source, target, small_sem.at[number]))
            small[-1].start()
        pl.semaphore_wait(barrier, sum(1 if cond is None else cond.astype(jnp.int32) for _, cond in partners))

        started = []

        def remote(src, dst, device, send_if=None, recv_if=None):
            number = len(started)
            copy = pltpu.make_async_remote_copy(
                src_ref=src, dst_ref=dst, send_sem=send_sem.at[number], recv_sem=recv_sem.at[number],
                device_id=device, device_id_type=MESH,
            )
            started.append((copy, send_if, recv_if))
            when(send_if, copy.start)
            return started[-1:]

        def arrive(copies):
            for copy, _, recv_if in copies:
                when(recv_if, copy.wait_recv)

        def send_z(below_src, below_dst, above_src, above_dst):
            return remote(below_src, below_dst, (group, down), has_down, has_up) + remote(
                above_src, above_dst, (group, up), has_up, has_down
            )

        def send_rows(edge, dst):
            return remote(edge.at[0], dst.at[0], (group - 1, slab), has_prev, has_next) + remote(
                edge.at[1], dst.at[1], (group + 1, slab), has_next, has_prev
            )

        rims = ((0, 16, has_next), (1, 6, has_prev))
        own = pl.ds(8, tile)
        cut_edges = lambda edge, at, pad_ref, plane: (
            edge.__setitem__((0, at), pad_ref[plane, 8:10, :]),
            edge.__setitem__((1, at), pad_ref[plane, tile + 6 : tile + 8, :]),
        )

        des_planes = send_z(
            design_in.at[pl.ds(0, 2)], des_z.at[1], design_in.at[pl.ds(planes - 2, 2)], des_z.at[0]
        )

        def face_copy(way, plane, where, part=None, stop=None, passed=None):
            cut = pl.ds(0, rows) if part is None else pl.ds(part * (rows // 2), rows // 2)
            if passed is not None:
                source = relay.at[passed]
            elif way == 0:
                source = disp.at[plane // 3, plane % 3, 0, cut]
            else:
                source = disp.at[half + plane // 3, plane % 3, planes - 1, cut]
            faces = (high_face, low_face)[way]
            return pltpu.make_async_remote_copy(
                src_ref=source,
                dst_ref=faces.at[plane // 3, plane % 3, cut] if stop is None else relay.at[stop],
                send_sem=face_send.at[way, plane // 3] if passed is None else relay_send.at[passed],
                recv_sem=face_recv.at[way, plane // 3] if stop is None else relay_recv.at[stop],
                device_id=(group, where),
                device_id_type=MESH,
            )

        def slot_copy(way, slot, where):
            return pltpu.make_async_remote_copy(
                src_ref=disp.at[slot, :, 0] if way == 0 else disp.at[half + slot, :, planes - 1],
                dst_ref=(high_face, low_face)[way].at[slot, :, pl.ds(0, rows)],
                send_sem=face_send.at[way, slot],
                recv_sem=face_recv.at[way, slot],
                device_id=(group, where),
                device_id_type=MESH,
            )

        ways = (
            (0, down, has_down, has_up, 0, run_down, run - 1),
            (1, up, has_up, has_down, RUN - 1, run_up, run + RUN),
        )
        for plane in (0, 1, 2, 5, 4, 3):
            for way, where, _, _, end, crosses, _ in ways:
                for part in range(2) if any((way, plane, k) in slots_of for k in range(2)) else (None,):
                    if (way, plane, part) in slots_of:
                        at, stop = slots_of[way, plane, part]
                        pl.when(crosses & (place == end))(face_copy(way, plane, run + at, part, stop).start)
                    else:
                        pl.when(crosses & (place == end))(face_copy(way, plane, where, part).start)
        for slot in range(half):
            for way, where, _, _, end, _, _ in ways:
                pl.when(place != end)(slot_copy(way, slot, where).start)

        def pass_on(turn):
            for way, _, _, _, _, crosses, target in ways:
                for (relay_way, plane, part), (at, stop) in slots_of.items():
                    if relay_way == way and (plane in FIRST[way]) == (turn == 0):

                        def forward():
                            face_copy(way, plane, target, part, stop).wait_recv()
                            face_copy(way, plane, target, part, passed=stop).start()

                        pl.when(crosses & (place == at))(forward)

        for copy in small:
            copy.wait()

        zero_rows = jnp.zeros((8, cols), jnp.float32)
        for comp in range(3):
            for slot in range(slots):
                for plane in range(planes):
                    field[slot, comp, plane, rows : rows + 8, :] = zero_rows
            for slot in range(half):
                low_face[slot, comp, rows : rows + 8, :] = zero_rows
                high_face[slot, comp, rows : rows + 8, :] = zero_rows

        def clear(face_ref):
            for slot in range(half):
                for comp in range(3):
                    face_ref[slot, comp, 0:rows, :] = jnp.zeros((rows, cols), jnp.float32)

        pl.when(slab == 0)(lambda: clear(low_face))
        pl.when(slab == slabs - 1)(lambda: clear(high_face))

        coef = []
        for slot in range(slots):
            node = slot_node[slot]
            index = jnp.clip(node, 0, node_weight.shape[0] - 1)
            value = node_weight[index] * node_stiffness[index]
            coef.append(jnp.where(node < node_weight.shape[0], value, 0.0))

        last = lax.broadcasted_iota(jnp.int32, (8, cols), 1) == cols - 1
        next_rows = lax.broadcasted_iota(jnp.int32, (8, cols), 0) == 0

        def modes_of(plane_ref, block):
            def load(comp):
                return [plane_ref[comp, pl.ds(pl.multiple_of((block + k) * 8, 8), 8), :] for k in range(2)]

            return plane_modes(load, next_rows, last)

        def keep(slot, block, modes):
            for comp in range(3):
                for mode in range(4):
                    kept[slot, comp, mode, pl.ds(pl.multiple_of(block * 8, 8), 8), :] = modes[comp][mode]

        def kept_modes(slot, block):
            span = pl.ds(pl.multiple_of(block * 8, 8), 8)
            return [[kept[slot, comp, mode, span, :] for mode in range(4)] for comp in range(3)]

        for slot in range(slots):
            loads[slot].wait()

            def block_step(block, carry):
                here = modes_of(field.at[slot, :, 0], block)
                if slot >= half:
                    keep(slot, block, here)
                for layer in range(planes - 1):
                    above = modes_of(field.at[slot, :, layer + 1], block)
                    value = coef[slot] * layer_energy(here, above)
                    spot = (lax.rem(block, 2), lax.div(block, 2), layer)
                    in_sums[spot] = value if slot == 0 else in_sums[spot] + value
                    here = above
                if slot < half:
                    keep(slot, block, here)
                return carry

            lax.fori_loop(0, rows // 8, block_step, 0, unroll=2)
            if slot < 2:
                pass_on(slot)

        def swap(sums, mate_sums):
            return remote(sums.at[1 - core], mate_sums, mate)

        def spread(sums, mate_sums, pair, peer_sums):
            for index in range(chips):
                pair[index] = sums[core, index] + mate_sums[index]
            copies = []
            for k in range(1, chips):
                copies += remote(pair.at[lax.rem(chip + k, chips)], peer_sums.at[k - 1], peers[k - 1])
            return copies

        def total(pair, peer_sums, layer):
            return pair[chip, layer] + add_up([peer_sums[k, layer] for k in range(chips - 1)])

        in_swap = swap(in_sums, in_mate)
        arrive(des_planes)
        des_pad[pl.ds(2, planes), own, :] = design[...]
        des_pad[pl.ds(0, 2), own, :] = jnp.where(has_down, des_z[0], 0.0)
        des_pad[pl.ds(planes + 2, 2), own, :] = jnp.where(has_up, des_z[1], 0.0)
        for plane in range(planes + 4):
            cut_edges(des_edge, plane, des_pad, plane)
        des_rows = send_rows(des_edge, des_y)


        arrive(des_rows)
        for rim, first, cond in rims:
            des_pad[:, pl.ds(first, 2), :] = jnp.where(cond, des_y[rim], 0.0)
        row_at = lax.broadcasted_iota(jnp.int32, (tile, cols), 0) + group * tile
        ones = []
        for dy in range(3):
            within = lambda y: jnp.where((y >= 0) & (y < groups * tile), 1.0, 0.0)
            ones.append(within(row_at) if dy == 0 else within(row_at - dy) + within(row_at + dy))
        base = math.tanh(BETA * ETA)
        scale = base + math.tanh(BETA * (1.0 - ETA))
        filt_rows = [row_sums(des_pad, p) for p in range(planes + 4)]
        for plane in range(planes):
            z = slab * planes + plane
            here = lambda d: jnp.where((z + d >= 0) & (z + d < slabs * planes), 1.0, 0.0)
            gains = [1.0, here(-1) + here(1), here(-2) + here(2)]
            cover = smooth([[v * gain for v in ones] for gain in gains], cols)
            filtered = smooth(z_sums(filt_rows, plane + 2), cols) / cover
            level = jnp.tanh(BETA * (filtered - ETA))
            projected = (base + level) / scale
            slope = BETA * (1.0 - level * level) / scale
            fac[plane] = (-3.0 * (1.0 - E_FLOOR)) * (projected * projected) * slope / cover
        factor = remote(fac.at[planes - 1], fac_low, (group, up), has_up, has_down)
        arrive(in_swap)
        in_spread = spread(in_sums, in_mate, in_pair, in_peers)

        def face_energy(slot):
            for way, where, _, recv_if, *_ in ways:
                pl.when(recv_if)(slot_copy(way, slot, where).wait_recv)

            def face_step(block, carry):
                spot = lambda layer: (lax.rem(block, 2), lax.div(block, 2), layer)
                lower = layer_energy(modes_of(low_face.at[slot], block), kept_modes(half + slot, block))
                value = coef[half + slot] * lower
                face_sums[spot(0)] = value if slot == 0 else face_sums[spot(0)] + value
                upper = layer_energy(kept_modes(slot, block), modes_of(high_face.at[slot], block))
                value = coef[slot] * upper
                face_sums[spot(1)] = value if slot == 0 else face_sums[spot(1)] + value
                return carry

            lax.fori_loop(0, rows // 8, face_step, 0, unroll=4)

        def top_energy():
            def top_step(block, carry):
                spot = (lax.rem(block, 2), lax.div(block, 2), 1)
                zero = jnp.zeros((8, cols), jnp.float32)
                for slot in range(half, slots):
                    modes = modes_of(field.at[slot, :, planes - 1], block)
                    face_sums[spot] += coef[slot] * layer_energy(modes, [(zero,) * 4] * 3)
                return carry

            lax.fori_loop(0, rows // 8, top_step, 0)

        face_energy(0)
        pl.when(slab == slabs - 1)(top_energy)

        for slot in range(1, half):
            face_energy(slot)
        face_swap = swap(face_sums, face_mate)

        def corners(edge, lower, upper, dst):
            copies = []
            for rim, step, send_if, recv_if in ((0, -1, has_prev, has_next), (1, 1, has_next, has_prev)):
                for part, side, where, send_s, recv_s in (
                    (lower, 1, down, has_down, has_up),
                    (upper, 0, up, has_up, has_down),
                ):
                    copies += remote(
                        edge.at[rim, part], dst[side].at[rim], (group + step, where), send_if & send_s, recv_if & recv_s
                    )
            return copies

        arrive(in_spread)
        inner = planes - 1
        for layer in range(inner):
            sen[layer] = total(in_pair, in_peers, layer) * fac[layer]
        sen_edge[0, 0:inner] = sen[:, 0:2, :]
        sen_edge[1, 0:inner] = sen[:, tile - 2 : tile, :]
        halo = send_z(sen.at[pl.ds(0, 2)], sen_high, sen.at[inner - 1], sen_low)
        halo += corners(sen_edge, pl.ds(0, 2), inner - 1, (sen_cl, sen_ch))

        arrive(face_swap)
        face_spread = spread(face_sums, face_mate, face_pair, face_peers)
        sen_pad[pl.ds(2, inner), own, :] = sen[...]
        arrive(factor)
        arrive(face_spread)
        late[0] = total(face_pair, face_peers, 0) * jnp.where(has_down, fac_low[...], 0.0)
        late[1] = total(face_pair, face_peers, 1) * fac[inner]
        late_halo = send_z(late.at[0], late_z.at[1], late.at[1], late_z.at[0])
        sen_edge[0, inner : inner + 2] = late[:, 0:2, :]
        sen_edge[1, inner : inner + 2] = late[:, tile - 2 : tile, :]
        late_halo += corners(sen_edge, inner, inner + 1, (late_c.at[0], late_c.at[1]))
        late_halo += send_rows(sen_edge, sen_y)

        arrive(halo)
        sen_pad[0, own, :] = jnp.where(has_down, sen_low[...], 0.0)
        sen_pad[pl.ds(planes + 2, 2), own, :] = jnp.where(has_up, sen_high[...], 0.0)
        for rim, first, cond in rims:
            span = pl.ds(first, 2)
            sen_pad[0, span, :] = jnp.where(cond & has_down, sen_cl[rim], 0.0)
            sen_pad[pl.ds(planes + 2, 2), span, :] = jnp.where(cond & has_up, sen_ch[rim], 0.0)
        arrive(late_halo)
        sen_pad[1, own, :] = jnp.where(has_down, late[0] + late_z[0], 0.0)
        sen_pad[planes + 1, own, :] = late[1] + jnp.where(has_up, late_z[1], 0.0)
        for rim, first, cond in rims:
            span = pl.ds(first, 2)
            sen_pad[1, span, :] = jnp.where(cond & has_down, sen_y[rim, inner] + late_c[0, rim], 0.0)
            sen_pad[pl.ds(2, inner), span, :] = jnp.where(cond, sen_y[rim, 0:inner], 0.0)
            sen_pad[planes + 1, span, :] = jnp.where(cond, sen_y[rim, inner + 1], 0.0) + jnp.where(
                cond & has_up, late_c[1, rim], 0.0
            )
        sens_rows = [row_sums(sen_pad, p) for p in range(planes + 4)]
        for plane in range(planes):
            out[plane] = smooth(z_sums(sens_rows, plane + 2), cols)

        for copy, send_if, _ in started:
            when(send_if, copy.wait_send)
        for slot in range(half):
            for way, where, send_if, *_ in ways:
                pl.when(send_if)(slot_copy(way, slot, where).wait_send)
        for way, where, _, _, _, crosses, _ in ways:
            for (relay_way, plane, part), (at, stop) in slots_of.items():
                if relay_way == way:
                    pl.when(crosses & (place == at))(face_copy(way, plane, where, part, passed=stop).wait_send)

    vmem = lambda *shape: pltpu.VMEM(shape, jnp.float32)
    copies = 2 + 2 + 1 + 2 * chips + 6 + 8
    inner = planes - 1
    scratch = [
        pltpu.SMEM((slots,), jnp.int32),
        pltpu.SMEM((nodes,), jnp.float32),
        pltpu.SMEM((nodes,), jnp.float32),
        vmem(planes, tile, cols),
        vmem(slots, 3, planes, rows + 8, cols),
        vmem(slots, 3, 4, rows, cols),
        vmem(half, 3, rows + 8, cols),
        vmem(half, 3, rows + 8, cols),
        vmem(stops, rows // 2, cols),
        vmem(planes + 4, 24, cols),
        vmem(2, 2, tile, cols),
        vmem(2, planes + 4, 2, cols),
        vmem(2, planes + 4, 2, cols),
        vmem(planes, tile, cols),
        vmem(tile, cols),
        vmem(2, chips, inner, tile, cols),
        vmem(chips, inner, tile, cols),
        vmem(chips, inner, tile, cols),
        vmem(chips - 1, inner, tile, cols),
        vmem(inner, tile, cols),
        vmem(planes + 4, 24, cols),
        vmem(tile, cols),
        vmem(2, tile, cols),
        vmem(2, 2, cols),
        vmem(2, 2, 2, cols),
        vmem(2, planes + 1, 2, cols),
        vmem(2, planes + 1, 2, cols),
        vmem(2, chips, 2, tile, cols),
        vmem(chips, 2, tile, cols),
        vmem(chips, 2, tile, cols),
        vmem(chips - 1, 2, tile, cols),
        vmem(2, tile, cols),
        vmem(2, tile, cols),
        vmem(2, 2, 2, cols),
        pltpu.SemaphoreType.DMA((slots,)),
        pltpu.SemaphoreType.DMA((4,)),
        pltpu.SemaphoreType.DMA((copies,)),
        pltpu.SemaphoreType.DMA((copies,)),
        pltpu.SemaphoreType.DMA((2, half)),
        pltpu.SemaphoreType.DMA((2, half)),
        pltpu.SemaphoreType.DMA((stops,)),
        pltpu.SemaphoreType.DMA((stops,)),
    ]
    return kernel, scratch


def solution(mesh):
    groups, slabs = mesh.shape["nodes"], mesh.shape["space"]

    def per_device(displacement, slot_node, node_weight, node_stiffness, design):
        slots, _, planes, rows, cols = displacement.shape
        kernel, scratch = make_kernel(groups, slabs, node_weight.shape[0], slots, planes, rows, cols, design.shape[1])
        return pl.pallas_call(
            kernel,
            out_shape=jax.ShapeDtypeStruct(design.shape, jnp.float32),
            in_specs=[pl.BlockSpec(memory_space=pltpu.HBM)] * 5,
            out_specs=pl.BlockSpec(memory_space=pltpu.VMEM),
            scratch_shapes=scratch,
            compiler_params=pltpu.CompilerParams(
                collective_id=0, has_side_effects=True, vmem_limit_bytes=60 * 2**20
            ),
            cost_estimate=pl.CostEstimate(flops=40_000_000, bytes_accessed=4_000_000, transcendentals=8192),
            name="sensitivity",
        )(displacement, slot_node, node_weight, node_stiffness, design)

    return jax.shard_map(
        per_device,
        mesh=mesh,
        in_specs=(
            P("nodes", None, "space", None, None),
            P("nodes"),
            P(),
            P(),
            P("space", "nodes", None),
        ),
        out_specs=P("space", "nodes", None),
        check_vma=False,
    )
```

```python
import math

import jax
import jax.numpy as jnp
from jax import lax
from jax.experimental import pallas as pl
from jax.experimental.pallas import tpu as pltpu
from jax.sharding import PartitionSpec as P

POISSON = 0.3
E_FLOOR = 0.001
BETA = 8.0
ETA = 0.5
RADIUS = 2.5
MESH = pl.DeviceIdType.MESH
RUN = 4
RELAY_DOWN = {(1, 0): 3, (1, 1): 3, (4, 0): 1, (3, 1): 3, (4, 1): 2, (2, 0): 1, (2, 1): 1, (5, 0): 2, (5, 1): 2}
RELAY_UP = {(1, 0): 0, (1, 1): 0, (4, 0): 0, (4, 1): 1, (2, 0): 2, (2, 1): 2, (5, 0): 1, (5, 1): 1}
FIRST = ({1, 2, 5}, {1})


def relay_slots():
    used, slots = {}, {}
    for way, relays in enumerate((RELAY_DOWN, RELAY_UP)):
        for (plane, part), at in relays.items():
            slots[way, plane, part] = (at, used.get(at, 0))
            used[at] = used.get(at, 0) + 1
    return slots, max(used.values())


def weight(dz, dy, dx):
    return max(0.0, RADIUS - math.sqrt(dz * dz + dy * dy + dx * dx))


def add_up(terms):
    total = None
    for term in terms:
        total = term if total is None else total + term
    return total


def next_lane(v, last):
    return jnp.where(last, 0.0, pltpu.roll(v, v.shape[1] - 1, 1))


def plane_modes(load, next_rows, last):
    modes = []
    for comp in range(3):
        here, below = load(comp)
        up = pltpu.roll(jnp.where(next_rows, below, here), 7, 0)
        ysum, ydif = up + here, up - here
        ysum_x, ydif_x = next_lane(ysum, last), next_lane(ydif, last)
        modes.append((ysum_x + ysum, ysum_x - ysum, ydif_x + ydif, ydif_x - ydif))
    return modes


def layer_energy(low, high):
    lam = POISSON / ((1.0 + POISSON) * (1.0 - 2.0 * POISSON))
    shear = 1.0 / (2.0 * (1.0 + POISSON))
    sums = [[lo + hi for lo, hi in zip(a, b)] for a, b in zip(low, high)]
    difs = [[hi - lo for lo, hi in zip(a, b)] for a, b in zip(low, high)]
    (_, ax, ay, axy), (_, bx, by, bxy), (_, cx, cy, cxy) = sums
    (az, azx, ayz, axyz), (bz, bzx, byz, bxyz), (cz, czx, cyz, cxyz) = difs
    sq = lambda v: v * v
    div = sq(ax + by + cz)
    diag = sq(ax) + sq(by) + sq(cz)
    skew = sq(ay + bx) + sq(az + cx) + sq(bz + cy)
    even = sq(bxy + czx) + sq(axy + cyz) + sq(azx + byz)
    odd = sq(bxy - czx) + sq(axy - cyz) + sq(azx - byz)
    mixed = sq(ayz + bzx) + sq(ayz + cxy) + sq(bzx + cxy)
    high_order = sq(axyz) + sq(bxyz) + sq(cxyz)
    return (
        (lam / 16.0) * div
        + (2.0 * shear / 16.0) * diag
        + (shear / 16.0) * skew
        + ((lam + 1.5 * shear) / 48.0) * even
        + (1.5 * shear / 48.0) * odd
        + (shear / 48.0) * mixed
        + ((lam + 4.0 * shear) / 144.0) * high_order
    )


def smooth(windows, cols):
    lanes = lax.broadcasted_iota(jnp.int32, windows[0][0].shape, 1)
    total = None
    for dx in range(3):
        part = add_up(
            [weight(i, j, dx) * windows[i][j] for i in range(3) for j in range(3) if weight(i, j, dx) > 0.0]
        )
        if dx > 0:
            right = jnp.where(lanes < cols - dx, pltpu.roll(part, cols - dx, 1), 0.0)
            left = jnp.where(lanes >= dx, pltpu.roll(part, dx, 1), 0.0)
            part = left + right
        total = part if total is None else total + part
    return total


def row_sums(field, plane):
    at = lambda first: field[plane, first : first + 8, :]
    return [at(8), at(7) + at(9), at(6) + at(10)]


def z_sums(rows, plane):
    return [
        rows[plane],
        [a + b for a, b in zip(rows[plane - 1], rows[plane + 1])],
        [a + b for a, b in zip(rows[plane - 2], rows[plane + 2])],
    ]


def make_kernel(groups, slabs, nodes, slots, planes, rows, cols, tile):
    half = slots // 2
    chips = groups // 2
    slots_of, stops = relay_slots()

    def kernel(
        disp, slot_node_in, node_weight_in, node_stiffness_in, design_in, out,
        slot_node, node_weight, node_stiffness, design, field, kept, low_face, high_face, relay,
        des_pad, des_z, des_edge, des_y, fac, fac_low,
        in_sums, in_mate, in_pair, in_peers, sen, sen_pad, sen_low, sen_high, sen_cl, sen_ch, sen_edge, sen_y,
        face_sums, face_mate, face_pair, face_peers, late, late_z, late_c,
        load_sem, small_sem, send_sem, recv_sem, face_send, face_recv, relay_send, relay_recv,
    ):
        group = lax.axis_index("nodes")
        slab = lax.axis_index("space")
        core = lax.rem(group, 2)
        chip = lax.div(group, 2)
        place = lax.rem(slab, RUN)
        run = slab - place
        down, up = slab - 1, slab + 1
        has_prev, has_next = group > 0, group < groups - 1
        has_down, has_up = slab > 0, slab < slabs - 1
        run_down, run_up = run > 0, run < slabs - RUN
        mate = (group + 1 - 2 * core, slab)
        peers = [(2 * lax.rem(chip + k, chips) + core, slab) for k in range(1, chips)]

        def when(condition, action):
            if condition is None:
                action()
            else:
                pl.when(condition)(action)

        aside = group + 2 * core - 1
        partners = [((group, down), run_down & (place == 0)), ((group, up), run_up & (place == RUN - 1))]
        partners += [((group, run + lax.rem(place + k, RUN)), None) for k in range(1, RUN)]
        partners += [(mate, None)] + [(peer, None) for peer in peers]
        partners.append(((aside, slab), (aside >= 0) & (aside < groups)))
        barrier = pltpu.get_barrier_semaphore()
        for device, cond in partners:
            when(cond, lambda: pl.semaphore_signal(barrier, inc=1, device_id=device, device_id_type=MESH))
        loads = []
        for slot in range(slots):
            load = pltpu.make_async_copy(
                disp.at[slot], field.at[slot, :, :, pl.ds(0, rows), :], load_sem.at[slot]
            )
            load.start()
            loads.append(load)
        small = []
        for number, (source, target) in enumerate(
            (
                (design_in, design),
                (slot_node_in, slot_node),
                (node_weight_in, node_weight),
                (node_stiffness_in, node_stiffness),
            )
        ):
            small.append(pltpu.make_async_copy(source, target, small_sem.at[number]))
            small[-1].start()
        pl.semaphore_wait(barrier, sum(1 if cond is None else cond.astype(jnp.int32) for _, cond in partners))

        started = []

        def remote(src, dst, device, send_if=None, recv_if=None):
            number = len(started)
            copy = pltpu.make_async_remote_copy(
                src_ref=src, dst_ref=dst, send_sem=send_sem.at[number], recv_sem=recv_sem.at[number],
                device_id=device, device_id_type=MESH,
            )
            started.append((copy, send_if, recv_if))
            when(send_if, copy.start)
            return started[-1:]

        def arrive(copies):
            for copy, _, recv_if in copies:
                when(recv_if, copy.wait_recv)

        def send_z(below_src, below_dst, above_src, above_dst):
            return remote(below_src, below_dst, (group, down), has_down, has_up) + remote(
                above_src, above_dst, (group, up), has_up, has_down
            )

        def send_rows(edge, dst):
            return remote(edge.at[0], dst.at[0], (group - 1, slab), has_prev, has_next) + remote(
                edge.at[1], dst.at[1], (group + 1, slab), has_next, has_prev
            )

        rims = ((0, 16, has_next), (1, 6, has_prev))
        own = pl.ds(8, tile)
        cut_edges = lambda edge, at, pad_ref, plane: (
            edge.__setitem__((0, at), pad_ref[plane, 8:10, :]),
            edge.__setitem__((1, at), pad_ref[plane, tile + 6 : tile + 8, :]),
        )

        des_planes = send_z(
            design_in.at[pl.ds(0, 2)], des_z.at[1], design_in.at[pl.ds(planes - 2, 2)], des_z.at[0]
        )

        def face_copy(way, plane, where, part=None, stop=None, passed=None):
            cut = pl.ds(0, rows) if part is None else pl.ds(part * (rows // 2), rows // 2)
            if passed is not None:
                source = relay.at[passed]
            elif way == 0:
                source = disp.at[plane // 3, plane % 3, 0, cut]
            else:
                source = disp.at[half + plane // 3, plane % 3, planes - 1, cut]
            faces = (high_face, low_face)[way]
            return pltpu.make_async_remote_copy(
                src_ref=source,
                dst_ref=faces.at[plane // 3, plane % 3, cut] if stop is None else relay.at[stop],
                send_sem=face_send.at[way, plane // 3] if passed is None else relay_send.at[passed],
                recv_sem=face_recv.at[way, plane // 3] if stop is None else relay_recv.at[stop],
                device_id=(group, where),
                device_id_type=MESH,
            )

        def slot_copy(way, slot, where):
            return pltpu.make_async_remote_copy(
                src_ref=disp.at[slot, :, 0] if way == 0 else disp.at[half + slot, :, planes - 1],
                dst_ref=(high_face, low_face)[way].at[slot, :, pl.ds(0, rows)],
                send_sem=face_send.at[way, slot],
                recv_sem=face_recv.at[way, slot],
                device_id=(group, where),
                device_id_type=MESH,
            )

        ways = (
            (0, down, has_down, has_up, 0, run_down, run - 1),
            (1, up, has_up, has_down, RUN - 1, run_up, run + RUN),
        )
        for plane in (0, 1, 2, 5, 4, 3):
            for way, where, _, _, end, crosses, _ in ways:
                for part in range(2) if any((way, plane, k) in slots_of for k in range(2)) else (None,):
                    if (way, plane, part) in slots_of:
                        at, stop = slots_of[way, plane, part]
                        pl.when(crosses & (place == end))(face_copy(way, plane, run + at, part, stop).start)
                    else:
                        pl.when(crosses & (place == end))(face_copy(way, plane, where, part).start)
        for slot in range(half):
            for way, where, _, _, end, _, _ in ways:
                pl.when(place != end)(slot_copy(way, slot, where).start)

        def pass_on(turn):
            for way, _, _, _, _, crosses, target in ways:
                for (relay_way, plane, part), (at, stop) in slots_of.items():
                    if relay_way == way and (plane in FIRST[way]) == (turn == 0):

                        def forward():
                            face_copy(way, plane, target, part, stop).wait_recv()
                            face_copy(way, plane, target, part, passed=stop).start()

                        pl.when(crosses & (place == at))(forward)

        for copy in small:
            copy.wait()

        zero_rows = jnp.zeros((8, cols), jnp.float32)
        for comp in range(3):
            for slot in range(slots):
                for plane in range(planes):
                    field[slot, comp, plane, rows : rows + 8, :] = zero_rows
            for slot in range(half):
                low_face[slot, comp, rows : rows + 8, :] = zero_rows
                high_face[slot, comp, rows : rows + 8, :] = zero_rows

        def clear(face_ref):
            for slot in range(half):
                for comp in range(3):
                    face_ref[slot, comp, 0:rows, :] = jnp.zeros((rows, cols), jnp.float32)

        pl.when(slab == 0)(lambda: clear(low_face))
        pl.when(slab == slabs - 1)(lambda: clear(high_face))

        coef = []
        for slot in range(slots):
            node = slot_node[slot]
            index = jnp.clip(node, 0, node_weight.shape[0] - 1)
            value = node_weight[index] * node_stiffness[index]
            coef.append(jnp.where(node < node_weight.shape[0], value, 0.0))

        last = lax.broadcasted_iota(jnp.int32, (8, cols), 1) == cols - 1
        next_rows = lax.broadcasted_iota(jnp.int32, (8, cols), 0) == 0

        def modes_of(plane_ref, block):
            def load(comp):
                return [plane_ref[comp, pl.ds(pl.multiple_of((block + k) * 8, 8), 8), :] for k in range(2)]

            return plane_modes(load, next_rows, last)

        def keep(slot, block, modes):
            for comp in range(3):
                for mode in range(4):
                    kept[slot, comp, mode, pl.ds(pl.multiple_of(block * 8, 8), 8), :] = modes[comp][mode]

        def kept_modes(slot, block):
            span = pl.ds(pl.multiple_of(block * 8, 8), 8)
            return [[kept[slot, comp, mode, span, :] for mode in range(4)] for comp in range(3)]

        for slot in range(slots):
            loads[slot].wait()

            def block_step(block, carry):
                here = modes_of(field.at[slot, :, 0], block)
                if slot >= half:
                    keep(slot, block, here)
                for layer in range(planes - 1):
                    above = modes_of(field.at[slot, :, layer + 1], block)
                    value = coef[slot] * layer_energy(here, above)
                    spot = (lax.rem(block, 2), lax.div(block, 2), layer)
                    in_sums[spot] = value if slot == 0 else in_sums[spot] + value
                    here = above
                if slot < half:
                    keep(slot, block, here)
                return carry

            lax.fori_loop(0, rows // 8, block_step, 0, unroll=2)
            if slot < 2:
                pass_on(slot)

        def swap(sums, mate_sums):
            return remote(sums.at[1 - core], mate_sums, mate)

        def spread(sums, mate_sums, pair, peer_sums):
            for index in range(chips):
                pair[index] = sums[core, index] + mate_sums[index]
            copies = []
            for k in range(1, chips):
                copies += remote(pair.at[lax.rem(chip + k, chips)], peer_sums.at[k - 1], peers[k - 1])
            return copies

        def total(pair, peer_sums, layer):
            return pair[chip, layer] + add_up([peer_sums[k, layer] for k in range(chips - 1)])

        in_swap = swap(in_sums, in_mate)
        arrive(des_planes)
        des_pad[pl.ds(2, planes), own, :] = design[...]
        des_pad[pl.ds(0, 2), own, :] = jnp.where(has_down, des_z[0], 0.0)
        des_pad[pl.ds(planes + 2, 2), own, :] = jnp.where(has_up, des_z[1], 0.0)
        for plane in range(planes + 4):
            cut_edges(des_edge, plane, des_pad, plane)
        des_rows = send_rows(des_edge, des_y)


        arrive(des_rows)
        for rim, first, cond in rims:
            des_pad[:, pl.ds(first, 2), :] = jnp.where(cond, des_y[rim], 0.0)
        row_at = lax.broadcasted_iota(jnp.int32, (tile, cols), 0) + group * tile
        ones = []
        for dy in range(3):
            within = lambda y: jnp.where((y >= 0) & (y < groups * tile), 1.0, 0.0)
            ones.append(within(row_at) if dy == 0 else within(row_at - dy) + within(row_at + dy))
        base = math.tanh(BETA * ETA)
        scale = base + math.tanh(BETA * (1.0 - ETA))
        filt_rows = [row_sums(des_pad, p) for p in range(planes + 4)]
        for plane in range(planes):
            z = slab * planes + plane
            here = lambda d: jnp.where((z + d >= 0) & (z + d < slabs * planes), 1.0, 0.0)
            gains = [1.0, here(-1) + here(1), here(-2) + here(2)]
            cover = smooth([[v * gain for v in ones] for gain in gains], cols)
            filtered = smooth(z_sums(filt_rows, plane + 2), cols) / cover
            level = jnp.tanh(BETA * (filtered - ETA))
            projected = (base + level) / scale
            slope = BETA * (1.0 - level * level) / scale
            fac[plane] = (-3.0 * (1.0 - E_FLOOR)) * (projected * projected) * slope / cover
        factor = remote(fac.at[planes - 1], fac_low, (group, up), has_up, has_down)
        arrive(in_swap)
        in_spread = spread(in_sums, in_mate, in_pair, in_peers)

        def face_energy(slot):
            for way, where, _, recv_if, *_ in ways:
                pl.when(recv_if)(slot_copy(way, slot, where).wait_recv)

            def face_step(block, carry):
                spot = lambda layer: (lax.rem(block, 2), lax.div(block, 2), layer)
                lower = layer_energy(modes_of(low_face.at[slot], block), kept_modes(half + slot, block))
                value = coef[half + slot] * lower
                face_sums[spot(0)] = value if slot == 0 else face_sums[spot(0)] + value
                upper = layer_energy(kept_modes(slot, block), modes_of(high_face.at[slot], block))
                value = coef[slot] * upper
                face_sums[spot(1)] = value if slot == 0 else face_sums[spot(1)] + value
                return carry

            lax.fori_loop(0, rows // 8, face_step, 0, unroll=4)

        def top_energy():
            def top_step(block, carry):
                spot = (lax.rem(block, 2), lax.div(block, 2), 1)
                zero = jnp.zeros((8, cols), jnp.float32)
                for slot in range(half, slots):
                    modes = modes_of(field.at[slot, :, planes - 1], block)
                    face_sums[spot] += coef[slot] * layer_energy(modes, [(zero,) * 4] * 3)
                return carry

            lax.fori_loop(0, rows // 8, top_step, 0)

        face_energy(0)
        pl.when(slab == slabs - 1)(top_energy)

        for slot in range(1, half):
            face_energy(slot)
        face_swap = swap(face_sums, face_mate)

        def corners(edge, lower, upper, dst):
            copies = []
            for rim, step, send_if, recv_if in ((0, -1, has_prev, has_next), (1, 1, has_next, has_prev)):
                for part, side, where, send_s, recv_s in (
                    (lower, 1, down, has_down, has_up),
                    (upper, 0, up, has_up, has_down),
                ):
                    copies += remote(
                        edge.at[rim, part], dst[side].at[rim], (group + step, where), send_if & send_s, recv_if & recv_s
                    )
            return copies

        arrive(in_spread)
        inner = planes - 1
        for layer in range(inner):
            sen[layer] = total(in_pair, in_peers, layer) * fac[layer]
        sen_edge[0, 0:inner] = sen[:, 0:2, :]
        sen_edge[1, 0:inner] = sen[:, tile - 2 : tile, :]
        halo = send_z(sen.at[pl.ds(0, 2)], sen_high, sen.at[inner - 1], sen_low)
        halo += corners(sen_edge, pl.ds(0, 2), inner - 1, (sen_cl, sen_ch))

        arrive(face_swap)
        face_spread = spread(face_sums, face_mate, face_pair, face_peers)
        sen_pad[pl.ds(2, inner), own, :] = sen[...]
        arrive(factor)
        arrive(face_spread)
        late[0] = total(face_pair, face_peers, 0) * jnp.where(has_down, fac_low[...], 0.0)
        late[1] = total(face_pair, face_peers, 1) * fac[inner]
        late_halo = send_z(late.at[0], late_z.at[1], late.at[1], late_z.at[0])
        sen_edge[0, inner : inner + 2] = late[:, 0:2, :]
        sen_edge[1, inner : inner + 2] = late[:, tile - 2 : tile, :]
        late_halo += corners(sen_edge, inner, inner + 1, (late_c.at[0], late_c.at[1]))
        late_halo += send_rows(sen_edge, sen_y)

        arrive(halo)
        sen_pad[0, own, :] = jnp.where(has_down, sen_low[...], 0.0)
        sen_pad[pl.ds(planes + 2, 2), own, :] = jnp.where(has_up, sen_high[...], 0.0)
        for rim, first, cond in rims:
            span = pl.ds(first, 2)
            sen_pad[0, span, :] = jnp.where(cond & has_down, sen_cl[rim], 0.0)
            sen_pad[pl.ds(planes + 2, 2), span, :] = jnp.where(cond & has_up, sen_ch[rim], 0.0)
        for copy, send_if, _ in started:
            when(send_if, copy.wait_send)
        for slot in range(half):
            for way, where, send_if, *_ in ways:
                pl.when(send_if)(slot_copy(way, slot, where).wait_send)
        for way, where, _, _, _, crosses, _ in ways:
            for (relay_way, plane, part), (at, stop) in slots_of.items():
                if relay_way == way:
                    pl.when(crosses & (place == at))(face_copy(way, plane, where, part, passed=stop).wait_send)
        arrive(late_halo)
        sen_pad[1, own, :] = jnp.where(has_down, late[0] + late_z[0], 0.0)
        sen_pad[planes + 1, own, :] = late[1] + jnp.where(has_up, late_z[1], 0.0)
        for rim, first, cond in rims:
            span = pl.ds(first, 2)
            sen_pad[1, span, :] = jnp.where(cond & has_down, sen_y[rim, inner] + late_c[0, rim], 0.0)
            sen_pad[pl.ds(2, inner), span, :] = jnp.where(cond, sen_y[rim, 0:inner], 0.0)
            sen_pad[planes + 1, span, :] = jnp.where(cond, sen_y[rim, inner + 1], 0.0) + jnp.where(
                cond & has_up, late_c[1, rim], 0.0
            )
        sens_rows = [row_sums(sen_pad, p) for p in range(planes + 4)]
        for plane in range(planes):
            out[plane] = smooth(z_sums(sens_rows, plane + 2), cols)

    vmem = lambda *shape: pltpu.VMEM(shape, jnp.float32)
    copies = 2 + 2 + 1 + 2 * chips + 6 + 8
    inner = planes - 1
    scratch = [
        pltpu.SMEM((slots,), jnp.int32),
        pltpu.SMEM((nodes,), jnp.float32),
        pltpu.SMEM((nodes,), jnp.float32),
        vmem(planes, tile, cols),
        vmem(slots, 3, planes, rows + 8, cols),
        vmem(slots, 3, 4, rows, cols),
        vmem(half, 3, rows + 8, cols),
        vmem(half, 3, rows + 8, cols),
        vmem(stops, rows // 2, cols),
        vmem(planes + 4, 24, cols),
        vmem(2, 2, tile, cols),
        vmem(2, planes + 4, 2, cols),
        vmem(2, planes + 4, 2, cols),
        vmem(planes, tile, cols),
        vmem(tile, cols),
        vmem(2, chips, inner, tile, cols),
        vmem(chips, inner, tile, cols),
        vmem(chips, inner, tile, cols),
        vmem(chips - 1, inner, tile, cols),
        vmem(inner, tile, cols),
        vmem(planes + 4, 24, cols),
        vmem(tile, cols),
        vmem(2, tile, cols),
        vmem(2, 2, cols),
        vmem(2, 2, 2, cols),
        vmem(2, planes + 1, 2, cols),
        vmem(2, planes + 1, 2, cols),
        vmem(2, chips, 2, tile, cols),
        vmem(chips, 2, tile, cols),
        vmem(chips, 2, tile, cols),
        vmem(chips - 1, 2, tile, cols),
        vmem(2, tile, cols),
        vmem(2, tile, cols),
        vmem(2, 2, 2, cols),
        pltpu.SemaphoreType.DMA((slots,)),
        pltpu.SemaphoreType.DMA((4,)),
        pltpu.SemaphoreType.DMA((copies,)),
        pltpu.SemaphoreType.DMA((copies,)),
        pltpu.SemaphoreType.DMA((2, half)),
        pltpu.SemaphoreType.DMA((2, half)),
        pltpu.SemaphoreType.DMA((stops,)),
        pltpu.SemaphoreType.DMA((stops,)),
    ]
    return kernel, scratch


def solution(mesh):
    groups, slabs = mesh.shape["nodes"], mesh.shape["space"]

    def per_device(displacement, slot_node, node_weight, node_stiffness, design):
        slots, _, planes, rows, cols = displacement.shape
        kernel, scratch = make_kernel(groups, slabs, node_weight.shape[0], slots, planes, rows, cols, design.shape[1])
        return pl.pallas_call(
            kernel,
            out_shape=jax.ShapeDtypeStruct(design.shape, jnp.float32),
            in_specs=[pl.BlockSpec(memory_space=pltpu.HBM)] * 5,
            out_specs=pl.BlockSpec(memory_space=pltpu.VMEM),
            scratch_shapes=scratch,
            compiler_params=pltpu.CompilerParams(
                collective_id=0, has_side_effects=True, vmem_limit_bytes=60 * 2**20
            ),
            cost_estimate=pl.CostEstimate(flops=40_000_000, bytes_accessed=4_000_000, transcendentals=8192),
            name="sensitivity",
        )(displacement, slot_node, node_weight, node_stiffness, design)

    return jax.shard_map(
        per_device,
        mesh=mesh,
        in_specs=(
            P("nodes", None, "space", None, None),
            P("nodes"),
            P(),
            P(),
            P("space", "nodes", None),
        ),
        out_specs=P("space", "nodes", None),
        check_vma=False,
    )
```
